512 devices in a mesh: fsdp: 64 (over x, z), tp: 8 (over y, core).
Axes of the slice: x: 4, y: 4, z: 16, core: 2. Of those that a mesh axis runs over, the one named last changes fastest.
Arguments:
- gradient: float32 [2, 8192, 8192], P(None, 'fsdp', 'tp'), may hold values from -16 to 16
- momentum: float32 [2, 8192, 8192], P(None, 'fsdp', 'tp'), may hold values from -6 to 6
- basis: float32 [2, 8192, 256], P(None, ('tp', 'fsdp')), may hold values from -1 to 1
Outputs:
- new_momentum: float32 [2, 8192, 8192], P(None, 'fsdp', 'tp')
- new_basis: float32 [2, 8192, 256], P(None, ('tp', 'fsdp'))
- update: float32 [2, 8192, 8192], P(None, 'fsdp', 'tp')
The draws below stay inside these ranges and needn't reach their ends.
All inputs are finite; a program needn't handle non-finite values.
Results may differ from the reference program's by a relative error of at most 0.0003.
Values sent between devices are 32-bit elements; how exact they have to be, the bound alone decides.
A program may use at most 64 MiB of HBM per device.

```python
import math
import jax
import jax.numpy as jnp
from jax import lax

ROWS = 8192
COLS = 8192
RANK = 256
LAYERS = 2


def draw_basis(key, part):
    key = jax.random.fold_in(key, 7)
    first_key, second_key, pick_key, size_key, scale_key = jax.random.split(key, 5)
    half = RANK // 2
    shape = (LAYERS, COLS, half)
    leading = jnp.clip(jax.random.normal(first_key, shape, jnp.float32), -4.0, 4.0)
    trailing = jnp.clip(jax.random.normal(second_key, shape, jnp.float32), -4.0, 4.0)
    spread = 0.8
    picked = jax.random.randint(pick_key, (LAYERS, 1, half), 0, 4) < 3
    lows = jnp.log(jnp.float32(0.006))
    highs = jnp.log(jnp.float32(0.02))
    offset = jnp.exp(lows + (highs - lows) * jax.random.uniform(size_key, (LAYERS, 1, half), jnp.float32))
    partner = jnp.where(picked, leading + offset * trailing, trailing)
    joined = jnp.stack([leading, partner], -1).reshape(LAYERS, COLS, RANK)
    column_scale = jnp.exp(jax.random.uniform(scale_key, (LAYERS, 1, RANK), jnp.float32, -spread, spread))
    return (joined * column_scale * COLS ** (-0.5)).astype(jnp.float32)


def strengthened(result, stream_key, source, target, blocks, factor):
    def block_of(dim):
        return (jnp.arange(result.shape[dim]) // (result.shape[dim] // blocks)).reshape((-1,) + (1,) * (result.ndim - 1 - dim))

    one_side = jax.random.permutation(stream_key, blocks)[block_of(target)]
    other_side = (block_of(target) + blocks // 2) % blocks
    return jnp.where((block_of(source) == one_side) | (block_of(source) == other_side), factor * result, result)


def block_scale(key, extent, pieces, smallest, largest):
    gain = 1.0
    for position, parts in pieces:
        draws = jax.random.uniform(jax.random.fold_in(jax.random.fold_in(key, 6), position), (parts,), jnp.float32, smallest / len(pieces), largest / len(pieces))
        gain = gain * jnp.repeat(jnp.exp(draws), extent[position] // parts).reshape((-1,) + (1,) * (len(extent) - 1 - position))
    return gain


def centred(rng, extent, scale, reach, cuts=(), dtype=jnp.bfloat16):
    gain = block_scale(rng, extent, cuts, -0.22, 0.18) if cuts else 1.0
    entries = jax.random.normal(rng, extent, jnp.float32) * scale * gain
    return jnp.minimum(jnp.maximum(entries, -reach), reach).astype(dtype)


def bell_draw_with(stream_key, shape, deviation, bound, shards, heavy, dtype=jnp.bfloat16):
    values = deviation * jax.random.normal(stream_key, shape, jnp.float32)
    if shards:
        values = values * block_scale(stream_key, shape, shards, -0.22, 0.18)
    return jnp.clip(strengthened(values, jax.random.fold_in(stream_key, 3), *heavy), -bound, bound).astype(dtype)


def setup_inputs(seed: int = 0) -> dict:
    key_of = jax.random.split(jax.random.key(seed), 4)
    return {
        "gradient": bell_draw_with(key_of[0], (LAYERS, ROWS, COLS), 1.0, 16.0, ((1, 64), (2, 8)), (1, 2, 64, 4.0), jnp.float32),
        "momentum": centred(key_of[1], (LAYERS, ROWS, COLS), 1.0, 6.0, ((1, 64), (2, 8)), jnp.float32),
        "basis": draw_basis(jax.random.fold_in(key_of[3], 71), 0),
    }


keep_rate = 0.95
eps = 1e-06

def one_matrix(gradient, momentum, basis):
    highest = lax.Precision.HIGHEST
    buffer = momentum + gradient
    product = jnp.dot(buffer.astype(jnp.float32), basis.astype(jnp.float32), precision=highest, preferred_element_type=jnp.float32)
    for sweep in range(2):
        gram = jnp.dot(product.T.astype(jnp.float32), product.astype(jnp.float32), precision=highest, preferred_element_type=jnp.float32)
        factor = jnp.linalg.cholesky(gram)
        product = jax.scipy.linalg.solve_triangular(factor, product.T, lower=True).T
    columns = jnp.dot(buffer.T.astype(jnp.float32), product.astype(jnp.float32), precision=highest, preferred_element_type=jnp.float32)
    new_momentum = buffer - (1.0 - keep_rate) * jnp.dot(product.astype(jnp.float32), columns.T.astype(jnp.float32), precision=highest, preferred_element_type=jnp.float32)
    normalized = columns / jnp.sqrt(lax.optimization_barrier(jnp.sum(columns * columns, 0)) + eps)[None, :]
    scale_factor = math.sqrt(ROWS * COLS / RANK)
    update = scale_factor * jnp.dot(product.astype(jnp.float32), normalized.T.astype(jnp.float32), precision=highest, preferred_element_type=jnp.float32)
    return (new_momentum, normalized, update)

def reference(gradient, momentum, basis):
    moms, bases, updates = ([], [], [])
    for layer in range(LAYERS):
        first, second, third = one_matrix(gradient[layer], momentum[layer], basis[layer])
        moms.append(first)
        bases.append(second)
        updates.append(third)
    return (jnp.stack(moms), jnp.stack(bases), jnp.stack(updates))
```

```python
import functools
import math

import jax
import jax.numpy as jnp
from jax import lax
from jax.experimental import pallas as pl
from jax.experimental.pallas import tpu as pltpu
from jax.sharding import PartitionSpec as P

ROWS = 8192
COLS = 8192
RANK = 256
LAYERS = 2
XS, ZS, YS, CS = 4, 16, 4, 2
TP = YS * CS
MESH = pl.DeviceIdType.MESH
HIGHEST = lax.Precision.HIGHEST
F32 = jnp.float32
BF16 = jnp.bfloat16
HALF = RANK // 2

keep_rate = 0.95
eps = 1e-06


def dot(a, b, dims):
    return lax.dot_general(a, b, (dims, ((), ())), precision=HIGHEST, preferred_element_type=F32)


class Place:
    def __init__(self):
        self.f = lax.axis_index("fsdp")
        self.t = lax.axis_index("tp")
        self.x = lax.div(self.f, ZS)
        self.z = lax.rem(self.f, ZS)
        self.y = lax.div(self.t, CS)
        self.c = lax.rem(self.t, CS)

    def zat(self, d):
        return lax.rem(self.z + (ZS + d), ZS)

    def xat(self, d):
        return lax.rem(self.x + (XS + d), XS)

    def yat(self, d):
        return lax.rem(self.y + (YS + d), YS)

    def zdev(self, d):
        return (self.x * ZS + self.zat(d), self.t)

    def xdev(self, d):
        return (self.xat(d) * ZS + self.z, self.t)

    def tdev(self, d):
        return (self.f, lax.rem(self.t + (TP + d), TP))

    def ydev(self, d):
        return (self.f, self.yat(d) * CS + self.c)

    def cdev(self):
        return (self.f, self.y * CS + (1 - self.c))


class Wires:
    def __init__(self, send, recv):
        self.send, self.recv, self.used = send, recv, 0
        self.sent = []

    def go(self, src, dst, device):
        i = self.used
        self.used += 1
        copy = pltpu.make_async_remote_copy(
            src_ref=src, dst_ref=dst, send_sem=self.send.at[i], recv_sem=self.recv.at[i],
            device_id=device, device_id_type=MESH,
        )
        copy.start()
        self.sent.append(copy)
        return copy

    def drain(self):
        for copy in self.sent:
            copy.wait_send()
        self.sent = []


def greet(devices):
    barrier = pltpu.get_barrier_semaphore()
    for device in devices:
        pl.semaphore_signal(barrier, inc=1, device_id=device, device_id_type=MESH)
    pl.semaphore_wait(barrier, len(devices))


def gather_plane(me, w, full):
    xa = [None] + [w.go(full.at[0, me.x, me.z], full.at[0, me.x, me.z], me.xdev(d)) for d in (1, 2, 3)]
    ring = {}
    plane = {}
    ahead = {}

    def spread(zd):
        block = full.at[1, me.x, me.zat(zd)]
        plane[zd] = [w.go(block, block, me.xdev(1)), w.go(block, block, me.xdev(-1))]

    def forward(zd):
        plane[zd][0].wait_recv()
        low = full.at[1, me.xat(-1), me.zat(zd), pl.ds(0, 8)]
        first = w.go(low, low, me.xdev(1))
        plane[zd][1].wait_recv()
        high = full.at[1, me.xat(1), me.zat(zd), pl.ds(8, 8)]
        ahead[zd] = [first, w.go(high, high, me.xdev(-1))]

    for s in range(9):
        for way, last in ((1, 8), (-1, 7)):
            if s > last:
                continue
            if s > 0:
                ring["b", way, s - 1].wait_recv()
            if s < last:
                block = full.at[1, me.x, me.zat(-way * s)]
                ring["b", way, s] = w.go(block, block, me.zdev(way))
        for zd in ([0] if s == 0 else [-s, s] if s < 8 else [-s]):
            spread(zd)
        for q in range(XS):
            for way, last in ((1, 8), (-1, 7)):
                if s > last:
                    continue
                if s == 0 and q > 0 and way == 1:
                    xa[q].wait_recv()
                if s > 0:
                    ring["a", way, s - 1, q].wait_recv()
                if s < last:
                    block = full.at[0, me.xat(-q), me.zat(-way * s)]
                    ring["a", way, s, q] = w.go(block, block, me.zdev(way))
        if s > 0:
            b = s - 1
            for zd in ([0] if b == 0 else [-b, b]):
                forward(zd)
    forward(-8)
    for pair in ahead.values():
        for copy in pair:
            copy.wait_recv()


def scatter_plane(me, w, part, full, rb0, xb0, rb1, half1, whole1):
    order = [8] + [d for s in range(7, 0, -1) for d in (s, -s)] + [0]
    slot = {d: i for i, d in enumerate(order)}
    first = {}
    for d in order:
        z = me.zat(d)
        i = slot[d]
        first[d] = [
            w.go(part.at[1, me.xat(2), z, pl.ds(0, 8)], half1.at[0, i], me.xdev(1)),
            w.go(part.at[1, me.xat(2), z, pl.ds(8, 8)], half1.at[1, i], me.xdev(-1)),
        ]
    second = {}

    def pass_on(d):
        z = me.zat(d)
        i = slot[d]
        first[d][0].wait_recv()
        part[1, me.xat(1), z, 0:8] = part[1, me.xat(1), z, 0:8] + half1[0, i]
        one = w.go(part.at[1, me.xat(1), z], whole1.at[0, i], me.xdev(1))
        first[d][1].wait_recv()
        part[1, me.xat(-1), z, 8:16] = part[1, me.xat(-1), z, 8:16] + half1[1, i]
        second[d] = [one, w.go(part.at[1, me.xat(-1), z], whole1.at[1, i], me.xdev(-1))]

    def collect(d):
        z = me.zat(d)
        i = slot[d]
        second[d][0].wait_recv()
        second[d][1].wait_recv()
        part[1, me.x, z] = part[1, me.x, z] + whole1[0, i] + whole1[1, i]

    def group(s):
        r = 8 - s
        return [8] if r == 8 else [0] if r == 0 else [r, -r]

    ring = {}
    for d in group(0):
        pass_on(d)
    for s in range(9):
        for q in range(XS):
            for k, (way, last) in enumerate(((1, 8), (-1, 7))):
                s0 = s - (8 - last)
                if s0 < 0 or s0 > last:
                    continue
                d = way * (last - s0)
                if s0 == 0:
                    ring["a", way, 0, q] = w.go(
                        part.at[0, q, me.zat(d)], rb0.at[k, 0, q], me.zdev(way))
                else:
                    ring["a", way, s0 - 1, q].wait_recv()
                    if s0 < last:
                        rb0[k, s0 - 1, q] = rb0[k, s0 - 1, q] + part[0, q, me.zat(d)]
                        ring["a", way, s0, q] = w.go(rb0.at[k, s0 - 1, q], rb0.at[k, s0, q], me.zdev(way))
        if s < 8:
            for d in group(s + 1):
                pass_on(d)
        for d in group(s):
            collect(d)
        for k, (way, last) in enumerate(((1, 8), (-1, 7))):
            s0 = s - (8 - last)
            if s0 < 0 or s0 > last:
                continue
            d = way * (last - s0)
            if s0 == 0:
                ring["b", way, 0] = w.go(part.at[1, me.x, me.zat(d)], rb1.at[k, 0], me.zdev(way))
            else:
                ring["b", way, s0 - 1].wait_recv()
                if s0 < last:
                    rb1[k, s0 - 1] = rb1[k, s0 - 1] + part[1, me.x, me.zat(d)]
                    ring["b", way, s0] = w.go(rb1.at[k, s0 - 1], rb1.at[k, s0], me.zdev(way))
    full[1, me.x, me.z] = part[1, me.x, me.z] + rb1[0, 7] + rb1[1, 6]
    for q in range(XS):
        rb0[0, 7, q] = rb0[0, 7, q] + part[0, q, me.z] + rb0[1, 6, q]
    copies = [w.go(rb0.at[0, 7, me.xat(d)], xb0.at[d], me.xdev(d)) for d in (1, 2, 3)]
    for copy in copies:
        copy.wait_recv()
    full[0, me.x, me.z] = rb0[0, 7, me.x] + xb0[1] + xb0[2] + xb0[3]


def sum_gram(me, w, product, gs, gfull, zbuf, xbuf, g_ref):
    gram = dot(product, product, ((0,), (0,)))
    for h in range(2):
        gs[h] = gram[:, h * HALF : (h + 1) * HALF].reshape(RANK // 8, 8, HALF)

    def tile(ref, z):
        return ref.at[lax.div(z, 8), me.y * 8 + lax.rem(z, 8)]

    copies = [w.go(tile(gs, me.zat(d)), zbuf.at[d], me.zdev(d)) for d in range(1, ZS)]
    total = gs[lax.div(me.z, 8), me.y * 8 + lax.rem(me.z, 8)]
    for d in range(1, ZS):
        copies[d - 1].wait_recv()
        total = total + zbuf[d]
    xbuf[me.x] = total
    copies = [w.go(xbuf.at[me.x], xbuf.at[me.x], me.xdev(d)) for d in range(1, XS)]
    for copy in copies:
        copy.wait_recv()
    gfull[lax.div(me.z, 8), me.y * 8 + lax.rem(me.z, 8)] = xbuf[0] + xbuf[1] + xbuf[2] + xbuf[3]
    copies = [w.go(tile(gfull, me.z), tile(gfull, me.z), me.zdev(d)) for d in range(1, ZS)]
    for copy in copies:
        copy.wait_recv()
    mine = gfull.at[:, pl.ds(me.y * 8, 8)]
    copies = [w.go(mine, mine, me.ydev(d)) for d in range(1, YS)]
    for copy in copies:
        copy.wait_recv()
    for h in range(2):
        g_ref[:, h * HALF : (h + 1) * HALF] = gfull[h].reshape(RANK, HALF)


def first_kernel(grad, mom, basis, p_ref, g_ref, gbuf, mbuf, full, part, rs, gs, gfull, zbuf, xbuf, send, recv, local):
    me = Place()
    w = Wires(send, recv)
    loads = [pltpu.make_async_copy(grad, gbuf, local.at[0]), pltpu.make_async_copy(mom, mbuf, local.at[1])]
    for load in loads:
        load.start()
    full[0, me.x, me.z] = basis[0]
    full[1, me.x, me.z] = basis[1]
    greet([me.zdev(d) for d in range(1, ZS)] + [me.xdev(d) for d in range(1, XS)] + [me.tdev(d) for d in range(1, TP)])
    gather_plane(me, w, full)
    for load in loads:
        load.wait()
    share = part.shape[2]
    for l in range(LAYERS):
        total = jnp.zeros((part.shape[1] * share, RANK), F32)
        for x in range(XS):
            cols = pl.ds(x * 256, 256)
            total = total + dot(
                mbuf[l, :, cols] + gbuf[l, :, cols], full[l, x].reshape(256, RANK), ((1,), (0,)))
        part[l] = total.reshape(part.shape[1], share, RANK)
    copies = []
    for d in range(1, TP):
        there = lax.rem(me.t + d, TP)
        copies.append(w.go(part.at[lax.rem(there, CS), lax.div(there, CS)], rs.at[d], me.tdev(d)))
    total = part[me.c, me.y]
    for d in range(1, TP):
        copies[d - 1].wait_recv()
        total = total + rs[d]
    rows = pl.ds(me.y * share, share)
    p_ref[rows] = total
    copies = [w.go(p_ref.at[rows], p_ref.at[rows], me.ydev(d)) for d in range(1, YS)]
    for copy in copies:
        copy.wait_recv()
    sum_gram(me, w, p_ref[...], gs, gfull, zbuf, xbuf, g_ref)
    w.drain()


def second_kernel(p, inv, p_ref, g_ref, gs, gfull, zbuf, xbuf, send, recv):
    me = Place()
    w = Wires(send, recv)
    p_ref[...] = dot(p[...], inv[...], ((1,), (1,)))
    greet([me.zdev(d) for d in range(1, ZS)] + [me.xdev(d) for d in range(1, XS)] + [me.ydev(d) for d in range(1, YS)])
    sum_gram(me, w, p_ref[...], gs, gfull, zbuf, xbuf, g_ref)
    w.drain()


def last_kernel(grad, mom, p, inv, new_mom, new_basis, update,
                gbuf, mbuf, q, part, full, rb0, xb0, rb1, half1, whole1, sq, send, recv, local):
    me = Place()
    w = Wires(send, recv)
    loads = [pltpu.make_async_copy(grad, gbuf, local.at[0]), pltpu.make_async_copy(mom, mbuf, local.at[1])]
    for load in loads:
        load.start()
    q[me.c] = dot(p[...], inv[...], ((1,), (1,)))
    greet([me.zdev(1), me.zdev(-1)] + [me.xdev(d) for d in range(1, XS)] + [me.tdev(d) for d in range(1, TP)])
    swap = w.go(q.at[me.c], q.at[me.c], me.cdev())
    for load in loads:
        load.wait()
    gbuf[...] = gbuf[...] + mbuf[...]
    swap.wait_recv()
    for l in range(LAYERS):
        for x in range(XS):
            cols = dot(gbuf[l, :, pl.ds(x * 256, 256)], q[l], ((0,), (0,)))
            part[l, x] = cols.reshape(ZS, 16, RANK)
    scatter_plane(me, w, part, full, rb0, xb0, rb1, half1, whole1)
    gather_plane(me, w, full)
    for l in range(LAYERS):
        squares = jnp.zeros((1, RANK), F32)
        for x in range(XS):
            block = full[l, x].reshape(256, RANK)
            squares = squares + jnp.sum(block * block, 0, keepdims=True)
        sq[me.t, l] = jnp.broadcast_to(squares, (8, RANK))
    copies = [w.go(sq.at[me.t], sq.at[me.t], me.tdev(d)) for d in range(1, TP)]
    for l in range(LAYERS):
        for x in range(XS):
            block = full[l, x].reshape(256, RANK)
            cols = pl.ds(x * 256, 256)
            new_mom[l, :, cols] = gbuf[l, :, cols] - (1.0 - keep_rate) * dot(q[l], block, ((1,), (1,)))
    for copy in copies:
        copy.wait_recv()
    for l in range(LAYERS):
        squares = sq[0, l]
        for t in range(1, TP):
            squares = squares + sq[t, l]
        norm = jnp.sqrt(squares[0:1] + eps)
        new_basis[l] = full[l, me.x, me.z] / norm
        scaled = q[l] * (math.sqrt(ROWS * COLS / RANK) / norm)
        for x in range(XS):
            block = full[l, x].reshape(256, RANK)
            update[l, :, pl.ds(x * 256, 256)] = dot(scaled, block, ((1,), (1,)))
    w.drain()


def split3(a):
    high = a.astype(BF16)
    rest = a - high.astype(F32)
    mid = rest.astype(BF16)
    low = (rest - mid.astype(F32)).astype(BF16)
    return high, mid, low


def eliminate(a_ref, w_ref):
    b = 32
    lanes = lax.broadcasted_iota(jnp.int32, (b, RANK), 1)
    rows = lax.broadcasted_iota(jnp.int32, (b, RANK), 0)
    row_index = lax.broadcasted_iota(jnp.int32, (b, 1), 0)
    for r0 in range(0, RANK, b):
        panel = a_ref[r0 : r0 + b, :]
        scale = jnp.zeros((b, 1), F32)
        for k in range(b):
            j = r0 + k
            col = panel[:, j : j + 1]
            pivot = panel[k : k + 1, j : j + 1]
            scale = jnp.where(row_index == k, lax.rsqrt(pivot), scale)
            ratio = jnp.where(row_index > k, col * (1.0 / pivot), 0.0)
            at = lanes == j
            row = jnp.where(at[0:1], 1.0, panel[k : k + 1, :])
            kept = jnp.where(at & (rows >= k), jnp.where(rows == k, 1.0, 0.0), panel)
            panel = kept - ratio * row
        panel = panel * scale
        done = lanes <= rows + r0
        w_ref[r0 : r0 + b, :] = jnp.where(done, panel, 0.0)
        if r0 + b < RANK:
            inner = (lanes >= r0) & (lanes < r0 + b) & (lanes > rows + r0)
            right = jnp.where(inner, 0.0, panel)
            h, m, l = split3(panel)
            hr, mr, lr = split3(right)
            left6 = jnp.concatenate([h, h, m, h, l, m], 0)
            right6 = jnp.concatenate([hr, mr, hr, lr, hr, mr], 0)
            rest = RANK - r0 - b
            change = lax.dot_general(
                left6, right6, (((0,), (0,)), ((), ())), preferred_element_type=F32)
            all_lanes = lax.broadcasted_iota(jnp.int32, (rest, RANK), 1)
            old = jnp.where((all_lanes >= r0) & (all_lanes < r0 + b), 0.0, a_ref[r0 + b :, :])
            a_ref[r0 + b :, :] = old - change[r0 + b :, :]


def factor_kernel(g, w_ref, a):
    a[...] = g[...]
    eliminate(a, w_ref)


def vmem(*shape):
    return pltpu.VMEM(shape, F32)


def params(collective_id):
    return pltpu.CompilerParams(collective_id=collective_id, has_side_effects=True, vmem_limit_bytes=48 * 2**20)


V = pl.BlockSpec(memory_space=pltpu.VMEM)
ANY = pl.BlockSpec(memory_space=pl.ANY)


def sums(n):
    return [
        vmem(2, RANK // 8, 8, HALF), vmem(2, RANK // 8, 8, HALF), vmem(ZS, 8, HALF), vmem(XS, 8, HALF),
        pltpu.SemaphoreType.DMA((n,)), pltpu.SemaphoreType.DMA((n,)),
    ]


def per_device(gradient, momentum, basis):
    rows, cols = gradient.shape[1:]
    share = basis.shape[1]
    small = jax.ShapeDtypeStruct((RANK, RANK), F32)
    tall = jax.ShapeDtypeStruct((rows, RANK), F32)
    product, gram = pl.pallas_call(
        first_kernel,
        out_shape=(tall, small),
        in_specs=[ANY, ANY, V],
        out_specs=(V, V),
        scratch_shapes=[
            vmem(LAYERS, rows, cols), vmem(LAYERS, rows, cols), vmem(LAYERS, XS, ZS, share, RANK),
            vmem(LAYERS, YS, rows // YS, RANK), vmem(TP, rows // YS, RANK),
        ] + sums(240) + [pltpu.SemaphoreType.DMA((2,))],
        compiler_params=params(0),
        name="first",
    )(gradient, momentum, basis)
    factor = pl.pallas_call(
        factor_kernel, out_shape=small, in_specs=[V], out_specs=V, scratch_shapes=[vmem(RANK, RANK)],
        compiler_params=pltpu.CompilerParams(vmem_limit_bytes=32 * 2**20), name="factor")
    inverse = factor(gram)
    product, gram = pl.pallas_call(
        second_kernel,
        out_shape=(tall, small),
        in_specs=[V, V],
        out_specs=(V, V),
        scratch_shapes=sums(40),
        compiler_params=params(1),
        name="second",
    )(product, inverse)
    inverse = factor(gram)
    whole = jax.ShapeDtypeStruct((LAYERS, rows, cols), F32)
    return pl.pallas_call(
        last_kernel,
        out_shape=(whole, jax.ShapeDtypeStruct((LAYERS, share, RANK), F32), whole),
        in_specs=[ANY, ANY, V, V],
        out_specs=(V, V, V),
        scratch_shapes=[
            vmem(LAYERS, rows, cols), vmem(LAYERS, rows, cols), vmem(LAYERS, rows, RANK),
            vmem(LAYERS, XS, ZS, share, RANK), vmem(LAYERS, XS, ZS, share, RANK),
            vmem(2, 8, XS, share, RANK), vmem(XS, share, RANK), vmem(2, 8, share, RANK),
            vmem(2, ZS, 8, RANK), vmem(2, ZS, share, RANK), vmem(TP, LAYERS, 8, RANK),
            pltpu.SemaphoreType.DMA((320,)), pltpu.SemaphoreType.DMA((320,)), pltpu.SemaphoreType.DMA((2,)),
        ],
        compiler_params=params(2),
        name="last",
    )(gradient, momentum, product, inverse)


def solution(mesh):
    return jax.shard_map(
        per_device,
        mesh=mesh,
        in_specs=(P(None, "fsdp", "tp"), P(None, "fsdp", "tp"), P(None, ("tp", "fsdp"), None)),
        out_specs=(P(None, "fsdp", "tp"), P(None, ("tp", "fsdp"), None), P(None, "fsdp", "tp")),
        check_vma=False,
    )
```

```python
import functools
import math

import jax
import jax.numpy as jnp
from jax import lax
from jax.experimental import pallas as pl
from jax.experimental.pallas import tpu as pltpu
from jax.sharding import PartitionSpec as P

ROWS = 8192
COLS = 8192
RANK = 256
LAYERS = 2
XS, ZS, YS, CS = 4, 16, 4, 2
TP = YS * CS
MESH = pl.DeviceIdType.MESH
HIGHEST = lax.Precision.HIGHEST
F32 = jnp.float32
BF16 = jnp.bfloat16
HALF = RANK // 2

keep_rate = 0.95
eps = 1e-06


def dot(a, b, dims):
    return lax.dot_general(a, b, (dims, ((), ())), precision=HIGHEST, preferred_element_type=F32)


def split2(a):
    high = a.astype(BF16)
    return high, (a - high.astype(F32)).astype(BF16)


def dot3(a, b, axis):
    ah, al = split2(a)
    bh, bl = split2(b)
    return lax.dot_general(
        jnp.concatenate([ah, ah, al], axis), jnp.concatenate([bh, bl, bh], axis),
        (((axis,), (axis,)), ((), ())), preferred_element_type=F32)


class Place:
    def __init__(self):
        self.f = lax.axis_index("fsdp")
        self.t = lax.axis_index("tp")
        self.x = lax.div(self.f, ZS)
        self.z = lax.rem(self.f, ZS)
        self.y = lax.div(self.t, CS)
        self.c = lax.rem(self.t, CS)

    def zat(self, d):
        return lax.rem(self.z + (ZS + d), ZS)

    def xat(self, d):
        return lax.rem(self.x + (XS + d), XS)

    def yat(self, d):
        return lax.rem(self.y + (YS + d), YS)

    def cols(self, e):
        return pl.ds(pl.multiple_of(self.xat(e) * 256, 256), 256)

    def zdev(self, d):
        return (self.x * ZS + self.zat(d), self.t)

    def xdev(self, d):
        return (self.xat(d) * ZS + self.z, self.t)

    def tdev(self, d):
        return (self.f, lax.rem(self.t + (TP + d), TP))

    def ydev(self, d):
        return (self.f, self.yat(d) * CS + self.c)

    def cdev(self):
        return (self.f, self.y * CS + (1 - self.c))


class Wires:
    def __init__(self, send, recv):
        self.send, self.recv, self.used = send, recv, 0
        self.sent = []

    def go(self, src, dst, device):
        i = self.used
        self.used += 1
        copy = pltpu.make_async_remote_copy(
            src_ref=src, dst_ref=dst, send_sem=self.send.at[i], recv_sem=self.recv.at[i],
            device_id=device, device_id_type=MESH,
        )
        copy.start()
        self.sent.append(copy)
        return copy

    def drain(self):
        for copy in self.sent:
            copy.wait_send()
        self.sent = []


def gathered(full0, full1, l, e):
    block = full0[:, e] if l == 0 else full1[e]
    return block.reshape(256, RANK)


def greet(devices):
    barrier = pltpu.get_barrier_semaphore()
    for device in devices:
        pl.semaphore_signal(barrier, inc=1, device_id=device, device_id_type=MESH)
    pl.semaphore_wait(barrier, len(devices))


WAYS = ((1, 8), (-1, 7))


def near(way, d):
    return 0 if d == 0 else 2 * d - 1 if way == 1 else 2 * d


def offset(slot):
    return 0 if slot == 0 else -((slot + 1) // 2) if slot % 2 else slot // 2


GROUPS = ((0, 5), (5, 9), (9, 13), (13, 16))


def gather_plane(me, w, own0, own1, full0, slots1, full1):
    full0[me.z, 0] = own0
    slots1[0, 0] = own1
    full1[0, me.z] = own1
    xa = {e: w.go(full0.at[me.z, 0], full0.at[me.z, (-e) % XS], me.xdev(e)) for e in (3, 1, 2)}
    ring, wide, ahead = {}, {}, {}

    def hop_b(s):
        for way, last in WAYS:
            if 0 < s <= last:
                ring["b", way, s - 1].wait_recv()
            if s < last:
                ring["b", way, s] = w.go(
                    slots1.at[0, near(way, s)], slots1.at[0, near(way, s + 1)], me.zdev(way))

    def hop_a(s):
        for half in (0, 1):
            pair = pl.ds(2 * half, 2)
            for way, last in WAYS:
                if s == 0 and way == 1:
                    for e in ((3,), (1, 2))[half]:
                        xa[e].wait_recv()
                if 0 < s <= last:
                    ring["a", way, s - 1, half].wait_recv()
                if s < last:
                    block = full0.at[me.zat(-way * s), pair]
                    ring["a", way, s, half] = w.go(block, block, me.zdev(way))

    def spread(g):
        lo, hi = GROUPS[g]
        group = slots1.at[0, pl.ds(lo, hi - lo)]
        wide[g] = [w.go(group, slots1.at[(-e) % XS, pl.ds(lo, hi - lo)], me.xdev(e)) for e in (1, -1)]
        for i in range(lo, hi):
            full1[0, me.zat(offset(i))] = slots1[0, i]

    def forward(g):
        lo, hi = GROUPS[g]
        mid = (lo + hi) // 2
        ahead[g] = []
        for n, (a, b, e) in enumerate(((lo, mid, 1), (mid, hi, -1))):
            wide[g][n].wait_recv()
            ahead[g].append(
                w.go(slots1.at[(-e) % XS, pl.ds(a, b - a)], slots1.at[2, pl.ds(a, b - a)], me.xdev(e)))
        for i in range(lo, hi):
            for e in (1, 3):
                full1[e, me.zat(offset(i))] = slots1[e, i]

    for s in range(9):
        hop_b(s)
        if s in (2, 4, 6, 8):
            spread(s // 2 - 1)
        hop_a(s)
        if s in (4, 6, 8):
            forward(s // 2 - 2)
    forward(3)
    for g in range(4):
        for copy in ahead[g]:
            copy.wait_recv()
        for i in range(*GROUPS[g]):
            full1[2, me.zat(offset(i))] = slots1[2, i]


FAR = [8] + [d for r in range(7, 0, -1) for d in (r, -r)] + [0]
FAR_GROUPS = ((0, 3), (3, 7), (7, 11), (11, 16))


def scatter_plane(me, w, part0, part1, rb0, xb0, rb1, half1, whole1):
    first, second, ring = {}, {}, {}

    def begin(g):
        lo, hi = FAR_GROUPS[g]
        mid = (lo + hi) // 2
        first[g] = [
            w.go(part1.at[2, pl.ds(a, b - a)], half1.at[pl.ds(a, b - a)], me.xdev(e))
            for a, b, e in ((lo, mid, 1), (mid, hi, -1))
        ]

    def pass_on(g):
        lo, hi = FAR_GROUPS[g]
        mid = (lo + hi) // 2
        second[g] = []
        for n, (a, b, e) in enumerate(((lo, mid, 1), (mid, hi, -1))):
            first[g][n].wait_recv()
            part1[e % XS, a:b] = part1[e % XS, a:b] + half1[a:b]
            second[g].append(
                w.go(part1.at[e % XS, pl.ds(lo, hi - lo)], whole1.at[n, pl.ds(lo, hi - lo)], me.xdev(e)))

    def collect(g):
        lo, hi = FAR_GROUPS[g]
        for copy in second[g]:
            copy.wait_recv()
        part1[0, lo:hi] = part1[0, lo:hi] + whole1[0, lo:hi] + whole1[1, lo:hi]

    def hop_a(s):
        for half in (0, 1):
            lo, hi = 2 * half, 2 * half + 2
            pair = pl.ds(lo, 2)
            for k, (way, last) in enumerate(WAYS):
                if s > last:
                    continue
                there = me.zat(way * (last - s))
                if s == 0:
                    ring["a", way, 0, half] = w.go(part0.at[there, pair], rb0.at[k, 0, pair], me.zdev(way))
                    continue
                ring["a", way, s - 1, half].wait_recv()
                if s < last:
                    rb0[k, s - 1, lo:hi] = rb0[k, s - 1, lo:hi] + part0[there, lo:hi]
                    ring["a", way, s, half] = w.go(rb0.at[k, s - 1, pair], rb0.at[k, s, pair], me.zdev(way))

    def hop_b(s):
        for k, (way, last) in enumerate(WAYS):
            if s > last:
                continue
            slot = FAR.index(way * (last - s))
            if s == 0:
                ring["b", way, 0] = w.go(part1.at[0, slot], rb1.at[k, 0], me.zdev(way))
                continue
            ring["b", way, s - 1].wait_recv()
            if s < last:
                rb1[k, s - 1] = rb1[k, s - 1] + part1[0, slot]
                ring["b", way, s] = w.go(rb1.at[k, s - 1], rb1.at[k, s], me.zdev(way))

    for g in range(4):
        begin(g)
    copies = []
    for s in range(11):
        if s <= 8:
            hop_a(s)
        if s == 8:
            rb0[0, 7] = rb0[0, 7] + part0[me.z] + rb0[1, 6]
            copies = [w.go(rb0.at[0, 7, e], xb0.at[e], me.xdev(e)) for e in (2, 1, 3)]
        if s in (0, 2, 4, 6):
            pass_on(s // 2)
        if s in (1, 3, 5, 7):
            collect(s // 2)
        if s >= 2:
            hop_b(s - 2)
    for copy in copies:
        copy.wait_recv()
    return rb0[0, 7, 0] + xb0[1] + xb0[2] + xb0[3], part1[0, 15] + rb1[0, 7] + rb1[1, 6]


def sum_gram(me, w, product, gs, gfull, zbuf, xbuf, g_ref):
    gram = dot(product, product, ((0,), (0,)))
    for h in range(2):
        gs[h] = gram[:, h * HALF : (h + 1) * HALF].reshape(RANK // 8, 8, HALF)

    def tile(ref, z):
        return ref.at[lax.div(z, 8), me.y * 8 + lax.rem(z, 8)]

    copies = [w.go(tile(gs, me.zat(d)), zbuf.at[d], me.zdev(d)) for d in range(1, ZS)]
    total = gs[lax.div(me.z, 8), me.y * 8 + lax.rem(me.z, 8)]
    for d in range(1, ZS):
        copies[d - 1].wait_recv()
        total = total + zbuf[d]
    xbuf[me.x] = total
    copies = [w.go(xbuf.at[me.x], xbuf.at[me.x], me.xdev(d)) for d in range(1, XS)]
    for copy in copies:
        copy.wait_recv()
    gfull[lax.div(me.z, 8), me.y * 8 + lax.rem(me.z, 8)] = xbuf[0] + xbuf[1] + xbuf[2] + xbuf[3]
    copies = [w.go(tile(gfull, me.z), tile(gfull, me.z), me.zdev(d)) for d in range(1, ZS)]
    for copy in copies:
        copy.wait_recv()
    mine = gfull.at[:, pl.ds(me.y * 8, 8)]
    copies = [w.go(mine, mine, me.ydev(d)) for d in range(1, YS)]
    for copy in copies:
        copy.wait_recv()
    for h in range(2):
        g_ref[:, h * HALF : (h + 1) * HALF] = gfull[h].reshape(RANK, HALF)


def first_kernel(grad, mom, basis, p_ref, g_ref, gbuf, mbuf, full0, slots1, full1, part, rs, gs, gfull, zbuf, xbuf, send, recv, local):
    me = Place()
    w = Wires(send, recv)
    loads = [pltpu.make_async_copy(grad, gbuf, local.at[0]), pltpu.make_async_copy(mom, mbuf, local.at[1])]
    for load in loads:
        load.start()
    greet([me.zdev(d) for d in range(1, ZS)] + [me.xdev(d) for d in range(1, XS)] + [me.tdev(d) for d in range(1, TP)])
    gather_plane(me, w, basis[0], basis[1], full0, slots1, full1)
    for load in loads:
        load.wait()
    share = part.shape[2]
    for l in range(LAYERS):
        total = jnp.zeros((part.shape[1] * share, RANK), F32)
        for e in range(XS):
            cols = me.cols(e)
            total = total + dot(
                mbuf[l, :, cols] + gbuf[l, :, cols], gathered(full0, full1, l, e), ((1,), (0,)))
        part[l] = total.reshape(part.shape[1], share, RANK)
    copies = []
    for d in range(1, TP):
        there = lax.rem(me.t + d, TP)
        copies.append(w.go(part.at[lax.rem(there, CS), lax.div(there, CS)], rs.at[d], me.tdev(d)))
    total = part[me.c, me.y]
    for d in range(1, TP):
        copies[d - 1].wait_recv()
        total = total + rs[d]
    rows = pl.ds(me.y * share, share)
    p_ref[rows] = total
    copies = [w.go(p_ref.at[rows], p_ref.at[rows], me.ydev(d)) for d in range(1, YS)]
    for copy in copies:
        copy.wait_recv()
    sum_gram(me, w, p_ref[...], gs, gfull, zbuf, xbuf, g_ref)
    w.drain()


def second_kernel(p, inv, p_ref, g_ref, gs, gfull, zbuf, xbuf, send, recv):
    me = Place()
    w = Wires(send, recv)
    p_ref[...] = dot(p[...], inv[...], ((1,), (1,)))
    greet([me.zdev(d) for d in range(1, ZS)] + [me.xdev(d) for d in range(1, XS)] + [me.ydev(d) for d in range(1, YS)])
    sum_gram(me, w, p_ref[...], gs, gfull, zbuf, xbuf, g_ref)
    w.drain()


def last_kernel(grad, mom, p, inv, new_mom, new_basis, update,
                gbuf, mbuf, q, part0, part1, tmp, full0, slots1, full1, rb0, xb0, rb1, half1, whole1, sq,
                send, recv, local):
    me = Place()
    w = Wires(send, recv)
    loads = [pltpu.make_async_copy(grad, gbuf, local.at[0]), pltpu.make_async_copy(mom, mbuf, local.at[1])]
    for load in loads:
        load.start()
    q[me.c] = dot(p[...], inv[...], ((1,), (1,)))
    greet([me.zdev(1), me.zdev(-1)] + [me.xdev(d) for d in range(1, XS)] + [me.tdev(d) for d in range(1, TP)])
    swap = w.go(q.at[me.c], q.at[me.c], me.cdev())
    for load in loads:
        load.wait()
    gbuf[...] = gbuf[...] + mbuf[...]
    swap.wait_recv()
    for e in (2, 1, 3, 0):
        tmp[...] = dot3(gbuf[1, :, me.cols(e)], q[1], 0).reshape(ZS, 16, RANK)
        for slot, d in enumerate(FAR):
            part1[e, slot] = tmp[me.zat(d)]
    for e in range(XS):
        part0[:, e] = dot3(gbuf[0, :, me.cols(e)], q[0], 0).reshape(ZS, 16, RANK)
    own = scatter_plane(me, w, part0, part1, rb0, xb0, rb1, half1, whole1)
    gather_plane(me, w, own[0], own[1], full0, slots1, full1)
    for l in range(LAYERS):
        squares = jnp.zeros((1, RANK), F32)
        for e in range(XS):
            block = gathered(full0, full1, l, e)
            squares = squares + jnp.sum(block * block, 0, keepdims=True)
        sq[me.t, l] = jnp.broadcast_to(squares, (8, RANK))
    copies = [w.go(sq.at[me.t], sq.at[me.t], me.tdev(d)) for d in range(1, TP)]
    for l in range(LAYERS):
        for e in range(XS):
            block = gathered(full0, full1, l, e)
            new_mom[l, :, me.cols(e)] = gbuf[l, :, me.cols(e)] - (1.0 - keep_rate) * dot3(q[l], block, 1)
    for copy in copies:
        copy.wait_recv()
    for l in range(LAYERS):
        squares = sq[0, l]
        for t in range(1, TP):
            squares = squares + sq[t, l]
        norm = jnp.sqrt(squares[0:1] + eps)
        new_basis[l] = own[l] / norm
        scaled = q[l] * (math.sqrt(ROWS * COLS / RANK) / norm)
        for e in range(XS):
            update[l, :, me.cols(e)] = dot3(scaled, gathered(full0, full1, l, e), 1)
    w.drain()


def split3(a):
    high = a.astype(BF16)
    rest = a - high.astype(F32)
    mid = rest.astype(BF16)
    low = (rest - mid.astype(F32)).astype(BF16)
    return high, mid, low


def eliminate(a_ref, w_ref):
    b = 32
    lane = lax.broadcasted_iota(jnp.int32, (8, HALF), 1)
    row = lax.broadcasted_iota(jnp.int32, (8, HALF), 0)
    for r0 in range(0, RANK, b):
        groups = b // 8
        panel = [[a_ref[r0 + 8 * g : r0 + 8 * g + 8, h * HALF : (h + 1) * HALF] for h in (0, 1)] for g in range(groups)]
        for g0 in range(groups):
            side, start = divmod(r0 + 8 * g0, HALF)
            cols = {
                (k, g): jnp.broadcast_to(panel[g][side][:, start + k : start + k + 1], (8, HALF))
                for k in range(8) for g in range(g0, groups)
            }
            scale = jnp.zeros((8, HALF), F32)
            for k in range(8):
                pivot = jnp.broadcast_to(cols[k, g0][k : k + 1], (8, HALF))
                inverse = 1.0 / pivot
                scale = jnp.where(row == k, lax.rsqrt(pivot), scale)
                ratio = {g: cols[k, g] * inverse for g in range(g0, groups)}
                ratio[g0] = jnp.where(row > k, ratio[g0], 0.0)
                for n in range(k + 1, 8):
                    spread = jnp.broadcast_to(cols[n, g0][k : k + 1], (8, HALF))
                    for g in range(g0, groups):
                        cols[n, g] = cols[n, g] - ratio[g] * spread
                at = lane == start + k
                for h in (0, 1):
                    spread = jnp.broadcast_to(panel[g0][h][k : k + 1], (8, HALF))
                    if h == side:
                        spread = jnp.where(at, 1.0, spread)
                    for g in range(g0, groups):
                        kept = panel[g][h]
                        if h == side and g == g0:
                            kept = jnp.where(at & (row >= k), jnp.where(row == k, 1.0, 0.0), kept)
                        elif h == side:
                            kept = jnp.where(at, 0.0, kept)
                        panel[g][h] = kept - ratio[g] * spread
            for h in (0, 1):
                panel[g0][h] = panel[g0][h] * scale
        whole = jnp.concatenate([jnp.concatenate(panel[g], 1) for g in range(groups)], 0)
        lanes = lax.broadcasted_iota(jnp.int32, (b, RANK), 1)
        rows = lax.broadcasted_iota(jnp.int32, (b, RANK), 0) + r0
        w_ref[r0 : r0 + b, :] = jnp.where(lanes <= rows, whole, 0.0)
        rest = r0 + b
        if rest < RANK:
            right = jnp.where((lanes > rows) & (lanes < rest), 0.0, whole)
            h, m, l = split3(whole)
            hr, mr, lr = split3(right)
            left = jnp.concatenate([h, h, m, h, l, m], 0)
            base = rest // HALF * HALF
            change = lax.dot_general(
                left[:, base:], jnp.concatenate([hr, mr, hr, lr, hr, mr], 0),
                (((0,), (0,)), ((), ())), preferred_element_type=F32)
            wide = lax.broadcasted_iota(jnp.int32, (RANK - rest, RANK), 1)
            old = jnp.where((wide >= r0) & (wide < rest), 0.0, a_ref[rest:, :])
            a_ref[rest:, :] = old - change[rest - base :, :]


def factor_kernel(g, w_ref, a):
    a[...] = g[...]
    eliminate(a, w_ref)


def refine_kernel(g, w_ref, a):
    lanes = lax.broadcasted_iota(jnp.int32, (RANK, RANK), 1)
    rows = lax.broadcasted_iota(jnp.int32, (RANK, RANK), 0)
    unit = jnp.where(lanes == rows, 1.0, 0.0)

    def lower(e):
        return jnp.where(lanes < rows, e, jnp.where(lanes == rows, 0.5 * e, 0.0))

    start = g[...] - unit
    w_ref[...] = unit - lower(start)

    def more(state):
        size, step = state
        return (size > 1e-6) & (step < 6)

    def newton(state):
        inv = w_ref[...]
        error = dot(dot(inv, g[...], ((1,), (0,))), inv, ((1,), (1,))) - unit
        w_ref[...] = inv - dot(lower(error), inv, ((1,), (0,)))
        return jnp.sum(error * error), state[1] + 1

    size, _ = lax.while_loop(more, newton, (jnp.sum(start * start), 0))

    @pl.when(jnp.logical_not(size <= 1e-6))
    def _():
        a[...] = g[...]
        eliminate(a, w_ref)


def vmem(*shape):
    return pltpu.VMEM(shape, F32)


def params(collective_id):
    return pltpu.CompilerParams(collective_id=collective_id, has_side_effects=True, vmem_limit_bytes=60 * 2**20)


V = pl.BlockSpec(memory_space=pltpu.VMEM)
ANY = pl.BlockSpec(memory_space=pl.ANY)


def sums(n):
    return [
        vmem(2, RANK // 8, 8, HALF), vmem(2, RANK // 8, 8, HALF), vmem(ZS, 8, HALF), vmem(XS, 8, HALF),
        pltpu.SemaphoreType.DMA((n,)), pltpu.SemaphoreType.DMA((n,)),
    ]


def per_device(gradient, momentum, basis):
    rows, cols = gradient.shape[1:]
    share = basis.shape[1]
    small = jax.ShapeDtypeStruct((RANK, RANK), F32)
    tall = jax.ShapeDtypeStruct((rows, RANK), F32)
    product, gram = pl.pallas_call(
        first_kernel,
        out_shape=(tall, small),
        in_specs=[ANY, ANY, V],
        out_specs=(V, V),
        scratch_shapes=[
            vmem(LAYERS, rows, cols), vmem(LAYERS, rows, cols),
            vmem(ZS, XS, share, RANK), vmem(XS, ZS, share, RANK), vmem(XS, ZS, share, RANK),
            vmem(LAYERS, YS, rows // YS, RANK), vmem(TP, rows // YS, RANK),
        ] + sums(128) + [pltpu.SemaphoreType.DMA((2,))],
        compiler_params=params(0),
        name="first",
    )(gradient, momentum, basis)
    def factor(kernel, gram):
        return pl.pallas_call(
            kernel, out_shape=small, in_specs=[V], out_specs=V, scratch_shapes=[vmem(RANK, RANK)],
            compiler_params=pltpu.CompilerParams(vmem_limit_bytes=32 * 2**20), name="factor")(gram)

    inverse = factor(factor_kernel, gram)
    product, gram = pl.pallas_call(
        second_kernel,
        out_shape=(tall, small),
        in_specs=[V, V],
        out_specs=(V, V),
        scratch_shapes=sums(40),
        compiler_params=params(1),
        name="second",
    )(product, inverse)
    inverse = factor(refine_kernel, gram)
    whole = jax.ShapeDtypeStruct((LAYERS, rows, cols), F32)
    return pl.pallas_call(
        last_kernel,
        out_shape=(whole, jax.ShapeDtypeStruct((LAYERS, share, RANK), F32), whole),
        in_specs=[ANY, ANY, V, V],
        out_specs=(V, V, V),
        scratch_shapes=[
            vmem(LAYERS, rows, cols), vmem(LAYERS, rows, cols), vmem(LAYERS, rows, RANK),
            vmem(ZS, XS, share, RANK), vmem(XS, ZS, share, RANK), vmem(ZS, share, RANK),
            vmem(ZS, XS, share, RANK), vmem(XS, ZS, share, RANK), vmem(XS, ZS, share, RANK),
            vmem(2, 8, XS, share, RANK), vmem(XS, share, RANK), vmem(2, 8, share, RANK),
            vmem(ZS, share, RANK), vmem(2, ZS, share, RANK), vmem(TP, LAYERS, 8, RANK),
            pltpu.SemaphoreType.DMA((140,)), pltpu.SemaphoreType.DMA((140,)), pltpu.SemaphoreType.DMA((2,)),
        ],
        compiler_params=params(2),
        name="last",
    )(gradient, momentum, product, inverse)


def solution(mesh):
    return jax.shard_map(
        per_device,
        mesh=mesh,
        in_specs=(P(None, "fsdp", "tp"), P(None, "fsdp", "tp"), P(None, ("tp", "fsdp"), None)),
        out_specs=(P(None, "fsdp", "tp"), P(None, ("tp", "fsdp"), None), P(None, "fsdp", "tp")),
        check_vma=False,
    )
```

```python
import math

import jax
import jax.numpy as jnp
from jax import lax
from jax.experimental import pallas as pl
from jax.experimental.pallas import tpu as pltpu
from jax.sharding import PartitionSpec as P

ROWS = 8192
COLS = 8192
RANK = 256
LAYERS = 2
XS, ZS, YS, CS = 4, 16, 4, 2
TP = YS * CS
MESH = pl.DeviceIdType.MESH
HIGHEST = lax.Precision.HIGHEST
F32 = jnp.float32
BF16 = jnp.bfloat16
HALF = RANK // 2

keep_rate = 0.95
eps = 1e-06


def dot(a, b, dims):
    return lax.dot_general(a, b, (dims, ((), ())), precision=HIGHEST, preferred_element_type=F32)


def split2(a):
    high = a.astype(BF16)
    return high, (a - high.astype(F32)).astype(BF16)


def dot3(a, b, axis):
    ah, al = split2(a)
    bh, bl = split2(b)
    return lax.dot_general(
        jnp.concatenate([ah, ah, al], axis), jnp.concatenate([bh, bl, bh], axis),
        (((axis,), (axis,)), ((), ())), preferred_element_type=F32)


class Place:
    def __init__(self):
        self.f = lax.axis_index("fsdp")
        self.t = lax.axis_index("tp")
        self.x = lax.div(self.f, ZS)
        self.z = lax.rem(self.f, ZS)
        self.y = lax.div(self.t, CS)
        self.c = lax.rem(self.t, CS)

    def zat(self, d):
        return lax.rem(self.z + (ZS + d), ZS)

    def xat(self, d):
        return lax.rem(self.x + (XS + d), XS)

    def yat(self, d):
        return lax.rem(self.y + (YS + d), YS)

    def cols(self, e):
        return pl.ds(pl.multiple_of(self.xat(e) * 256, 256), 256)

    def zdev(self, d):
        return (self.x * ZS + self.zat(d), self.t)

    def xdev(self, d):
        return (self.xat(d) * ZS + self.z, self.t)

    def tdev(self, d):
        return (self.f, lax.rem(self.t + (TP + d), TP))

    def ydev(self, d):
        return (self.f, self.yat(d) * CS + self.c)

    def cdev(self):
        return (self.f, self.y * CS + (1 - self.c))


class Wires:
    def __init__(self, send, recv):
        self.send, self.recv, self.used = send, recv, 0
        self.sent = []

    def go(self, src, dst, device):
        i = self.used
        self.used += 1
        copy = pltpu.make_async_remote_copy(
            src_ref=src, dst_ref=dst, send_sem=self.send.at[i], recv_sem=self.recv.at[i],
            device_id=device, device_id_type=MESH,
        )
        copy.start()
        self.sent.append(copy)
        return copy

    def drain(self):
        for copy in self.sent:
            copy.wait_send()
        self.sent = []


def gathered(full0, full1, l, e):
    block = full0[:, e] if l == 0 else full1[e]
    return block.reshape(256, RANK)


def greet(devices):
    barrier = pltpu.get_barrier_semaphore()
    for device in devices:
        pl.semaphore_signal(barrier, inc=1, device_id=device, device_id_type=MESH)
    pl.semaphore_wait(barrier, len(devices))


WAYS = ((1, 8), (-1, 7))


def near(way, d):
    return 0 if d == 0 else 2 * d - 1 if way == 1 else 2 * d


def offset(slot):
    return 0 if slot == 0 else -((slot + 1) // 2) if slot % 2 else slot // 2


GROUPS = ((0, 5), (5, 9), (9, 13), (13, 16))


def gather_plane(me, w, own0, own1, full0, slots1, full1, beside):
    full0[me.z, 0] = own0
    slots1[0, 0] = own1
    full1[0, me.z] = own1
    xa = {e: w.go(full0.at[me.z, 0], full0.at[me.z, (-e) % XS], me.xdev(e)) for e in (3, 1, 2)}
    ring, wide, ahead = {}, {}, {}

    def hop_b(s):
        for way, last in WAYS:
            if 0 < s <= last:
                ring["b", way, s - 1].wait_recv()
            if s < last:
                ring["b", way, s] = w.go(
                    slots1.at[0, near(way, s)], slots1.at[0, near(way, s + 1)], me.zdev(way))

    def hop_a(s):
        for half in (0, 1):
            pair = pl.ds(2 * half, 2)
            for way, last in WAYS:
                if s == 0 and way == 1:
                    for e in ((3,), (1, 2))[half]:
                        xa[e].wait_recv()
                if 0 < s <= last:
                    ring["a", way, s - 1, half].wait_recv()
                if s < last:
                    block = full0.at[me.zat(-way * s), pair]
                    ring["a", way, s, half] = w.go(block, block, me.zdev(way))

    def spread(g):
        lo, hi = GROUPS[g]
        group = slots1.at[0, pl.ds(lo, hi - lo)]
        wide[g] = [w.go(group, slots1.at[(-e) % XS, pl.ds(lo, hi - lo)], me.xdev(e)) for e in (1, -1)]
        for i in range(lo, hi):
            full1[0, me.zat(offset(i))] = slots1[0, i]

    def forward(g):
        lo, hi = GROUPS[g]
        mid = (lo + hi) // 2
        ahead[g] = []
        for n, (a, b, e) in enumerate(((lo, mid, 1), (mid, hi, -1))):
            wide[g][n].wait_recv()
            ahead[g].append(
                w.go(slots1.at[(-e) % XS, pl.ds(a, b - a)], slots1.at[2, pl.ds(a, b - a)], me.xdev(e)))
        for i in range(lo, hi):
            for e in (1, 3):
                full1[e, me.zat(offset(i))] = slots1[e, i]

    for s in range(9):
        hop_b(s)
        if s in (2, 4, 6, 8):
            spread(s // 2 - 1)
        hop_a(s)
        if s in (4, 6, 8):
            forward(s // 2 - 2)
        beside(s)
    forward(3)
    for g in range(4):
        for copy in ahead[g]:
            copy.wait_recv()
        for i in range(*GROUPS[g]):
            full1[2, me.zat(offset(i))] = slots1[2, i]


FAR = [8] + [d for r in range(7, 0, -1) for d in (r, -r)] + [0]
FAR_GROUPS = ((0, 3), (3, 7), (7, 11), (11, 16))


def scatter_plane(me, w, part0, part1, rb0, xb0, rb1, half1, whole1, beside):
    first, second, ring = {}, {}, {}

    def begin(g):
        lo, hi = FAR_GROUPS[g]
        mid = (lo + hi) // 2
        first[g] = [
            w.go(part1.at[2, pl.ds(a, b - a)], half1.at[pl.ds(a, b - a)], me.xdev(e))
            for a, b, e in ((lo, mid, 1), (mid, hi, -1))
        ]

    def pass_on(g):
        lo, hi = FAR_GROUPS[g]
        mid = (lo + hi) // 2
        second[g] = []
        for n, (a, b, e) in enumerate(((lo, mid, 1), (mid, hi, -1))):
            first[g][n].wait_recv()
            part1[e % XS, a:b] = part1[e % XS, a:b] + half1[a:b]
            second[g].append(
                w.go(part1.at[e % XS, pl.ds(lo, hi - lo)], whole1.at[n, pl.ds(lo, hi - lo)], me.xdev(e)))

    def collect(g):
        lo, hi = FAR_GROUPS[g]
        for copy in second[g]:
            copy.wait_recv()
        part1[0, lo:hi] = part1[0, lo:hi] + whole1[0, lo:hi] + whole1[1, lo:hi]

    def hop_a(s):
        for half in (0, 1):
            lo, hi = 2 * half, 2 * half + 2
            pair = pl.ds(lo, 2)
            for k, (way, last) in enumerate(WAYS):
                if s > last:
                    continue
                there = me.zat(way * (last - s))
                if s == 0:
                    ring["a", way, 0, half] = w.go(part0.at[there, pair], rb0.at[k, 0, pair], me.zdev(way))
                    continue
                ring["a", way, s - 1, half].wait_recv()
                if s < last:
                    rb0[k, s - 1, lo:hi] = rb0[k, s - 1, lo:hi] + part0[there, lo:hi]
                    ring["a", way, s, half] = w.go(rb0.at[k, s - 1, pair], rb0.at[k, s, pair], me.zdev(way))

    def hop_b(s):
        for k, (way, last) in enumerate(WAYS):
            if s > last:
                continue
            slot = FAR.index(way * (last - s))
            if s == 0:
                ring["b", way, 0] = w.go(part1.at[0, slot], rb1.at[k, 0], me.zdev(way))
                continue
            ring["b", way, s - 1].wait_recv()
            if s < last:
                rb1[k, s - 1] = rb1[k, s - 1] + part1[0, slot]
                ring["b", way, s] = w.go(rb1.at[k, s - 1], rb1.at[k, s], me.zdev(way))

    for g in range(4):
        begin(g)
    copies = []
    for s in range(11):
        if s <= 8:
            hop_a(s)
        if s == 8:
            rb0[0, 7] = rb0[0, 7] + part0[me.z] + rb0[1, 6]
            copies = [w.go(rb0.at[0, 7, e], xb0.at[e], me.xdev(e)) for e in (2, 1, 3)]
        if s in (0, 2, 4, 6):
            pass_on(s // 2)
        if s in (1, 3, 5, 7):
            collect(s // 2)
        if s >= 2:
            hop_b(s - 2)
        beside(s)
    for copy in copies:
        copy.wait_recv()
    return rb0[0, 7, 0] + xb0[1] + xb0[2] + xb0[3], part1[0, 15] + rb1[0, 7] + rb1[1, 6]


def sum_gram(me, w, product, gs, gfull, zbuf, xbuf):
    gram = dot(product, product, ((0,), (0,)))
    for h in range(2):
        gs[h] = gram[:, h * HALF : (h + 1) * HALF].reshape(RANK // 8, 8, HALF)

    def tile(ref, z):
        return ref.at[lax.div(z, 8), me.y * 8 + lax.rem(z, 8)]

    far = [8] + [d for r in range(7, 0, -1) for d in (r, ZS - r)]
    copies = [w.go(tile(gs, me.zat(d)), zbuf.at[d], me.zdev(d)) for d in far]
    yield
    total = gs[lax.div(me.z, 8), me.y * 8 + lax.rem(me.z, 8)]
    for d, copy in reversed(list(zip(far, copies))):
        copy.wait_recv()
        total = total + zbuf[d]
    xbuf[me.x] = total
    copies = [w.go(xbuf.at[me.x], xbuf.at[me.x], me.xdev(d)) for d in (2, 1, 3)]
    yield
    for copy in copies:
        copy.wait_recv()
    gfull[lax.div(me.z, 8), me.y * 8 + lax.rem(me.z, 8)] = xbuf[0] + xbuf[1] + xbuf[2] + xbuf[3]
    copies = [w.go(tile(gfull, me.z), tile(gfull, me.z), me.zdev(d)) for d in far]
    yield
    for copy in reversed(copies):
        copy.wait_recv()
    mine = gfull.at[:, pl.ds(me.y * 8, 8)]
    copies = [w.go(mine, mine, me.ydev(d)) for d in (2, 1, 3)]
    yield
    for copy in copies:
        copy.wait_recv()


def kernel(grad, mom, basis, new_mom, new_basis, update,
           gbuf, mbuf, bfull0, bslots1, bfull1, part, rs, p, q, a, w1, w2,
           gs, gfull, zbuf, xbuf, gs2, gfull2, zbuf2, xbuf2,
           part0, part1, tmp, full0, slots1, full1, rb0, xb0, rb1, half1, whole1, sq,
           send, recv, local):
    me = Place()
    w = Wires(send, recv)
    loads = [pltpu.make_async_copy(grad, gbuf, local.at[0]), pltpu.make_async_copy(mom, mbuf, local.at[1])]
    for load in loads:
        load.start()
    greet([me.zdev(d) for d in range(1, ZS)] + [me.xdev(d) for d in range(1, XS)] + [me.tdev(d) for d in range(1, TP)])

    def load_buffer(s):
        if s == 0:
            for load in loads:
                load.wait()
            gbuf[...] = gbuf[...] + mbuf[...]

    gather_plane(me, w, basis[0], basis[1], bfull0, bslots1, bfull1, load_buffer)

    share = part.shape[2]
    for l in range(LAYERS):
        total = jnp.zeros((part.shape[1] * share, RANK), F32)
        for e in range(XS):
            total = total + dot(gbuf[l, :, me.cols(e)], gathered(bfull0, bfull1, l, e), ((1,), (0,)))
        part[l] = total.reshape(part.shape[1], share, RANK)
    copies = []
    for d in range(1, TP):
        there = lax.rem(me.t + d, TP)
        copies.append(w.go(part.at[lax.rem(there, CS), lax.div(there, CS)], rs.at[d], me.tdev(d)))
    total = part[me.c, me.y]
    for d in range(1, TP):
        copies[d - 1].wait_recv()
        total = total + rs[d]
    rows = pl.ds(me.y * share, share)
    p[rows] = total
    copies = [w.go(p.at[rows], p.at[rows], me.ydev(d)) for d in (2, 1, 3)]
    for copy in copies:
        copy.wait_recv()

    for _ in sum_gram(me, w, p[...], gs, gfull, zbuf, xbuf):
        pass
    for h in range(2):
        a[:, h * HALF : (h + 1) * HALF] = gfull[h].reshape(RANK, HALF)
    for r0 in range(0, RANK, PANEL):
        eliminate(a, w1, r0)
    q[me.c] = dot(p[...], w1[...], ((1,), (1,)))
    swap = w.go(q.at[me.c], q.at[me.c], me.cdev())

    second = sum_gram(me, w, q[me.c], gs2, gfull2, zbuf2, xbuf2)
    next(second)
    swap.wait_recv()
    for e in (2, 1, 3, 0):
        tmp[...] = dot3(gbuf[1, :, me.cols(e)], q[1], 0).reshape(ZS, 16, RANK)
        for slot, d in enumerate(FAR):
            part1[e, slot] = tmp[me.zat(d)]
    for e in range(XS):
        part0[:, e] = dot3(gbuf[0, :, me.cols(e)], q[0], 0).reshape(ZS, 16, RANK)

    def go_on(s):
        if s in (2, 4, 7, 10):
            next(second, None)

    own = scatter_plane(me, w, part0, part1, rb0, xb0, rb1, half1, whole1, go_on)
    for h in range(2):
        a[:, h * HALF : (h + 1) * HALF] = gfull2[h].reshape(RANK, HALF)
    trade = []

    def factor_on(s):
        if s < 8:
            eliminate(a, w2.at[me.c], s * PANEL)
        if s == 7:
            trade.append(w.go(w2.at[me.c], w2.at[me.c], me.cdev()))

    gather_plane(me, w, own[0], own[1], full0, slots1, full1, factor_on)
    trade[0].wait_recv()
    w.drain()
    for l in range(LAYERS):
        q[l] = dot(q[l], w2[l], ((1,), (1,)))
        squares = jnp.zeros((1, RANK), F32)
        for e in range(XS):
            block = dot3(gathered(full0, full1, l, e), w2[l], 1)
            if l == 0:
                part0[:, e] = block.reshape(ZS, 16, RANK)
            else:
                part1[e] = block.reshape(ZS, 16, RANK)
            squares = squares + jnp.sum(block * block, 0, keepdims=True)
        sq[me.t, l] = jnp.broadcast_to(squares, (8, RANK))
    copies = [w.go(sq.at[me.t], sq.at[me.t], me.tdev(d)) for d in range(1, TP)]
    for l in range(LAYERS):
        for e in range(XS):
            block = gathered(part0, part1, l, e)
            new_mom[l, :, me.cols(e)] = gbuf[l, :, me.cols(e)] - (1.0 - keep_rate) * dot3(q[l], block, 1)
    for copy in copies:
        copy.wait_recv()
    for l in range(LAYERS):
        squares = sq[0, l]
        for t in range(1, TP):
            squares = squares + sq[t, l]
        norm = jnp.sqrt(squares[0:1] + eps)
        new_basis[l] = (part0[me.z, 0] if l == 0 else part1[0, me.z]) / norm
        scaled = q[l] * (math.sqrt(ROWS * COLS / RANK) / norm)
        for e in range(XS):
            update[l, :, me.cols(e)] = dot3(scaled, gathered(part0, part1, l, e), 1)
    w.drain()


PANEL = 32


def split3(a):
    high = a.astype(BF16)
    rest = a - high.astype(F32)
    mid = rest.astype(BF16)
    low = (rest - mid.astype(F32)).astype(BF16)
    return high, mid, low


def eliminate(a_ref, w_ref, r0):
    halves = [a_ref[r0 : r0 + PANEL, h * HALF : (h + 1) * HALF] for h in (0, 1)]
    finished = []
    for j0 in range(r0, r0 + PANEL, 8):
        side, start = divmod(j0, HALF)
        height = r0 + PANEL - j0
        lane = lax.broadcasted_iota(jnp.int32, (height, HALF), 1)
        row = lax.broadcasted_iota(jnp.int32, (height, HALF), 0)
        cols = [jnp.broadcast_to(halves[side][:, start + k : start + k + 1], (height, HALF)) for k in range(8)]
        scale = jnp.zeros((8, HALF), F32)
        for k in range(8):
            pivot = cols[k][k : k + 1]
            ratio = jnp.where(row > k, cols[k] * (1.0 / pivot), 0.0)
            scale = jnp.where(row[:8] == k, lax.rsqrt(pivot), scale)
            for n in range(k + 1, 8):
                cols[n] = cols[n] - ratio * cols[n][k : k + 1]
            for h in (0, 1):
                kept, spread = halves[h], halves[h][k : k + 1]
                if h == side:
                    spread = jnp.where(lane[0:1] == start + k, 1.0, spread)
                    kept = jnp.where((lane == start + k) & (row >= k), jnp.where(row == k, 1.0, 0.0), kept)
                halves[h] = kept - ratio * spread
        finished.append([half[:8] * scale for half in halves])
        halves = [half[8:] for half in halves] if height > 8 else None
    whole = jnp.concatenate([jnp.concatenate(rows, 1) for rows in finished], 0)
    lanes = lax.broadcasted_iota(jnp.int32, (PANEL, RANK), 1)
    rows = lax.broadcasted_iota(jnp.int32, (PANEL, RANK), 0) + r0
    w_ref[r0 : r0 + PANEL, :] = jnp.where(lanes <= rows, whole, 0.0)
    rest = r0 + PANEL
    if rest < RANK:
        right = jnp.where((lanes > rows) & (lanes < rest), 0.0, whole)
        h, m, l = split3(whole)
        hr, mr, lr = split3(right)
        left = jnp.concatenate([h, h, m, h, l, m], 0)
        base = rest // HALF * HALF
        change = lax.dot_general(
            left[:, base:], jnp.concatenate([hr, mr, hr, lr, hr, mr], 0),
            (((0,), (0,)), ((), ())), preferred_element_type=F32)
        wide = lax.broadcasted_iota(jnp.int32, (RANK - rest, RANK), 1)
        old = jnp.where((wide >= r0) & (wide < rest), 0.0, a_ref[rest:, :])
        a_ref[rest:, :] = old - change[rest - base :, :]


def vmem(*shape):
    return pltpu.VMEM(shape, F32)


V = pl.BlockSpec(memory_space=pltpu.VMEM)
ANY = pl.BlockSpec(memory_space=pl.ANY)
COPIES = 288


def per_device(gradient, momentum, basis):
    rows, cols = gradient.shape[1:]
    share = basis.shape[1]
    whole = jax.ShapeDtypeStruct((LAYERS, rows, cols), F32)
    plane = [vmem(ZS, XS, share, RANK), vmem(XS, ZS, share, RANK), vmem(XS, ZS, share, RANK)]
    sums = [vmem(2, RANK // 8, 8, HALF), vmem(2, RANK // 8, 8, HALF), vmem(ZS, 8, HALF), vmem(XS, 8, HALF)]
    return pl.pallas_call(
        kernel,
        out_shape=(whole, jax.ShapeDtypeStruct((LAYERS, share, RANK), F32), whole),
        in_specs=[ANY, ANY, V],
        out_specs=(V, V, V),
        scratch_shapes=[
            vmem(LAYERS, rows, cols), vmem(LAYERS, rows, cols), *plane,
            vmem(LAYERS, YS, rows // YS, RANK), vmem(TP, rows // YS, RANK), vmem(rows, RANK),
            vmem(LAYERS, rows, RANK), vmem(RANK, RANK), vmem(RANK, RANK), vmem(LAYERS, RANK, RANK),
            *sums, *sums,
            vmem(ZS, XS, share, RANK), vmem(XS, ZS, share, RANK), vmem(ZS, share, RANK), *plane,
            vmem(2, 8, XS, share, RANK), vmem(XS, share, RANK), vmem(2, 8, share, RANK),
            vmem(ZS, share, RANK), vmem(2, ZS, share, RANK), vmem(TP, LAYERS, 8, RANK),
            pltpu.SemaphoreType.DMA((COPIES,)), pltpu.SemaphoreType.DMA((COPIES,)), pltpu.SemaphoreType.DMA((2,)),
        ],
        compiler_params=pltpu.CompilerParams(
            collective_id=0, has_side_effects=True, vmem_limit_bytes=60 * 2**20),
        name="step",
    )(gradient, momentum, basis)


def solution(mesh):
    return jax.shard_map(
        per_device,
        mesh=mesh,
        in_specs=(P(None, "fsdp", "tp"), P(None, "fsdp", "tp"), P(None, ("tp", "fsdp"), None)),
        out_specs=(P(None, "fsdp", "tp"), P(None, ("tp", "fsdp"), None), P(None, "fsdp", "tp")),
        check_vma=False,
    )
```

```python
import math

import jax
import jax.numpy as jnp
from jax import lax
from jax.experimental import pallas as pl
from jax.experimental.pallas import tpu as pltpu
from jax.sharding import PartitionSpec as P

ROWS = 8192
COLS = 8192
RANK = 256
LAYERS = 2
XS, ZS, YS, CS = 4, 16, 4, 2
TP = YS * CS
MESH = pl.DeviceIdType.MESH
HIGHEST = lax.Precision.HIGHEST
F32 = jnp.float32
BF16 = jnp.bfloat16
HALF = RANK // 2

keep_rate = 0.95
eps = 1e-06


def dot(a, b, dims):
    return lax.dot_general(a, b, (dims, ((), ())), precision=HIGHEST, preferred_element_type=F32)


def split2(a):
    high = a.astype(BF16)
    return high, (a - high.astype(F32)).astype(BF16)


def dot3(a, b, axis):
    ah, al = split2(a)
    bh, bl = split2(b)
    return lax.dot_general(
        jnp.concatenate([ah, ah, al], axis), jnp.concatenate([bh, bl, bh], axis),
        (((axis,), (axis,)), ((), ())), preferred_element_type=F32)


class Place:
    def __init__(self):
        self.f = lax.axis_index("fsdp")
        self.t = lax.axis_index("tp")
        self.x = lax.div(self.f, ZS)
        self.z = lax.rem(self.f, ZS)
        self.y = lax.div(self.t, CS)
        self.c = lax.rem(self.t, CS)

    def zat(self, d):
        return lax.rem(self.z + (ZS + d), ZS)

    def xat(self, d):
        return lax.rem(self.x + (XS + d), XS)

    def yat(self, d):
        return lax.rem(self.y + (YS + d), YS)

    def cols(self, e):
        return pl.ds(pl.multiple_of(self.xat(e) * 256, 256), 256)

    def zdev(self, d):
        return (self.x * ZS + self.zat(d), self.t)

    def xdev(self, d):
        return (self.xat(d) * ZS + self.z, self.t)

    def tdev(self, d):
        return (self.f, lax.rem(self.t + (TP + d), TP))

    def ydev(self, d):
        return (self.f, self.yat(d) * CS + self.c)

    def cdev(self):
        return (self.f, self.y * CS + (1 - self.c))


class Wires:
    def __init__(self, send, recv):
        self.send, self.recv, self.used = send, recv, 0
        self.sent = []

    def go(self, src, dst, device):
        i = self.used
        self.used += 1
        copy = pltpu.make_async_remote_copy(
            src_ref=src, dst_ref=dst, send_sem=self.send.at[i], recv_sem=self.recv.at[i],
            device_id=device, device_id_type=MESH,
        )
        copy.start()
        self.sent.append(copy)
        return copy

    def drain(self):
        for copy in self.sent:
            copy.wait_send()
        self.sent = []


def gathered(full0, full1, l, e):
    block = full0[:, e] if l == 0 else full1[e]
    return block.reshape(256, RANK)


def greet(devices):
    barrier = pltpu.get_barrier_semaphore()
    for device in devices:
        pl.semaphore_signal(barrier, inc=1, device_id=device, device_id_type=MESH)
    pl.semaphore_wait(barrier, len(devices))


WAYS = ((1, 8), (-1, 7))


def near(way, d):
    return 0 if d == 0 else 2 * d - 1 if way == 1 else 2 * d


def offset(slot):
    return 0 if slot == 0 else -((slot + 1) // 2) if slot % 2 else slot // 2


GROUPS = ((0, 5), (5, 9), (9, 13), (13, 16))


def gather_plane(me, w, own0, own1, full0, slots1, full1, beside):
    full0[me.z, 0] = own0
    slots1[0, 0] = own1
    full1[0, me.z] = own1
    xa = {e: w.go(full0.at[me.z, 0], full0.at[me.z, (-e) % XS], me.xdev(e)) for e in (3, 1, 2)}
    ring, wide, ahead = {}, {}, {}

    def hop_b(s):
        for way, last in WAYS:
            if 0 < s <= last:
                ring["b", way, s - 1].wait_recv()
            if s < last:
                ring["b", way, s] = w.go(
                    slots1.at[0, near(way, s)], slots1.at[0, near(way, s + 1)], me.zdev(way))

    def hop_a(s):
        for half in (0, 1):
            pair = pl.ds(2 * half, 2)
            for way, last in WAYS:
                if s == 0 and way == 1:
                    for e in ((3,), (1, 2))[half]:
                        xa[e].wait_recv()
                if 0 < s <= last:
                    ring["a", way, s - 1, half].wait_recv()
                if s < last:
                    block = full0.at[me.zat(-way * s), pair]
                    ring["a", way, s, half] = w.go(block, block, me.zdev(way))

    def spread(g):
        lo, hi = GROUPS[g]
        group = slots1.at[0, pl.ds(lo, hi - lo)]
        wide[g] = [w.go(group, slots1.at[(-e) % XS, pl.ds(lo, hi - lo)], me.xdev(e)) for e in (1, -1)]
        for i in range(lo, hi):
            full1[0, me.zat(offset(i))] = slots1[0, i]

    def forward(g):
        lo, hi = GROUPS[g]
        mid = (lo + hi) // 2
        ahead[g] = []
        for n, (a, b, e) in enumerate(((lo, mid, 1), (mid, hi, -1))):
            wide[g][n].wait_recv()
            ahead[g].append(
                w.go(slots1.at[(-e) % XS, pl.ds(a, b - a)], slots1.at[2, pl.ds(a, b - a)], me.xdev(e)))
        for i in range(lo, hi):
            for e in (1, 3):
                full1[e, me.zat(offset(i))] = slots1[e, i]

    for s in range(9):
        hop_b(s)
        if s in (2, 4, 6, 8):
            spread(s // 2 - 1)
        hop_a(s)
        if s in (4, 6, 8):
            forward(s // 2 - 2)
        beside(s)
    forward(3)
    for g in range(4):
        for copy in ahead[g]:
            copy.wait_recv()
        for i in range(*GROUPS[g]):
            full1[2, me.zat(offset(i))] = slots1[2, i]


FAR = [8] + [d for r in range(7, 0, -1) for d in (r, -r)] + [0]
FAR_GROUPS = ((0, 3), (3, 7), (7, 11), (11, 16))


def scatter_plane(me, w, part0, part1, rb0, xb0, rb1, half1, whole1, fill0, fill1, beside):
    first, second, ring = {}, {}, {}

    def begin(g):
        lo, hi = FAR_GROUPS[g]
        mid = (lo + hi) // 2
        first[g] = [
            w.go(part1.at[2, pl.ds(a, b - a)], half1.at[pl.ds(a, b - a)], me.xdev(e))
            for a, b, e in ((lo, mid, 1), (mid, hi, -1))
        ]

    def pass_on(g):
        lo, hi = FAR_GROUPS[g]
        mid = (lo + hi) // 2
        second[g] = []
        for n, (a, b, e) in enumerate(((lo, mid, 1), (mid, hi, -1))):
            first[g][n].wait_recv()
            part1[e % XS, a:b] = part1[e % XS, a:b] + half1[a:b]
            second[g].append(
                w.go(part1.at[e % XS, pl.ds(lo, hi - lo)], whole1.at[n, pl.ds(lo, hi - lo)], me.xdev(e)))

    def collect(g):
        lo, hi = FAR_GROUPS[g]
        for copy in second[g]:
            copy.wait_recv()
        part1[0, lo:hi] = part1[0, lo:hi] + whole1[0, lo:hi] + whole1[1, lo:hi]

    def hop_a(s):
        for half in (0, 1):
            lo, hi = 2 * half, 2 * half + 2
            pair = pl.ds(lo, 2)
            for k, (way, last) in enumerate(WAYS):
                if s > last:
                    continue
                there = me.zat(way * (last - s))
                if s == 0:
                    ring["a", way, 0, half] = w.go(part0.at[there, pair], rb0.at[k, 0, pair], me.zdev(way))
                    continue
                ring["a", way, s - 1, half].wait_recv()
                if s < last:
                    rb0[k, s - 1, lo:hi] = rb0[k, s - 1, lo:hi] + part0[there, lo:hi]
                    ring["a", way, s, half] = w.go(rb0.at[k, s - 1, pair], rb0.at[k, s, pair], me.zdev(way))

    def hop_b(s):
        for k, (way, last) in enumerate(WAYS):
            if s > last:
                continue
            slot = FAR.index(way * (last - s))
            if s == 0:
                ring["b", way, 0] = w.go(part1.at[0, slot], rb1.at[k, 0], me.zdev(way))
                continue
            ring["b", way, s - 1].wait_recv()
            if s < last:
                rb1[k, s - 1] = rb1[k, s - 1] + part1[0, slot]
                ring["b", way, s] = w.go(rb1.at[k, s - 1], rb1.at[k, s], me.zdev(way))

    fill1(2)
    for g in range(4):
        begin(g)
    fill0()
    copies = []
    for s in range(11):
        if s <= 8:
            hop_a(s)
        if s == 0:
            fill1(1)
            fill1(3)
        if s == 1:
            fill1(0)
        if s == 8:
            rb0[0, 7] = rb0[0, 7] + part0[me.z] + rb0[1, 6]
            copies = [w.go(rb0.at[0, 7, e], xb0.at[e], me.xdev(e)) for e in (2, 1, 3)]
        if s in (0, 2, 4, 6):
            pass_on(s // 2)
        if s in (1, 3, 5, 7):
            collect(s // 2)
        if s >= 2:
            hop_b(s - 2)
        beside(s)
    for copy in copies:
        copy.wait_recv()
    return rb0[0, 7, 0] + xb0[1] + xb0[2] + xb0[3], part1[0, 15] + rb1[0, 7] + rb1[1, 6]


def sum_gram(me, w, product, gs, gfull, zbuf, xbuf):
    gram = dot(product, product, ((0,), (0,)))
    for h in range(2):
        gs[h] = gram[:, h * HALF : (h + 1) * HALF].reshape(RANK // 8, 8, HALF)

    def tile(ref, z):
        return ref.at[lax.div(z, 8), me.y * 8 + lax.rem(z, 8)]

    far = [8] + [d for r in range(7, 0, -1) for d in (r, ZS - r)]
    copies = [w.go(tile(gs, me.zat(d)), zbuf.at[d], me.zdev(d)) for d in far]
    yield
    total = gs[lax.div(me.z, 8), me.y * 8 + lax.rem(me.z, 8)]
    for d, copy in reversed(list(zip(far, copies))):
        copy.wait_recv()
        total = total + zbuf[d]
    xbuf[me.x] = total
    copies = [w.go(xbuf.at[me.x], xbuf.at[me.x], me.xdev(d)) for d in (2, 1, 3)]
    yield
    for copy in copies:
        copy.wait_recv()
    gfull[lax.div(me.z, 8), me.y * 8 + lax.rem(me.z, 8)] = xbuf[0] + xbuf[1] + xbuf[2] + xbuf[3]
    copies = [w.go(tile(gfull, me.z), tile(gfull, me.z), me.zdev(d)) for d in far]
    yield
    for copy in reversed(copies):
        copy.wait_recv()
    mine = gfull.at[:, pl.ds(me.y * 8, 8)]
    copies = [w.go(mine, mine, me.ydev(d)) for d in (2, 1, 3)]
    yield
    for copy in copies:
        copy.wait_recv()


def kernel(grad, mom, basis, new_mom, new_basis, update,
           gbuf, mbuf, bfull0, bslots1, bfull1, part, rs, q, p1, p2, a, w1, w2, wide,
           gs, gfull, zbuf, xbuf, gs2, gfull2, zbuf2, xbuf2,
           part0, part1, tmp, full0, slots1, full1, rb0, xb0, rb1, half1, whole1, cols0, cols1, sq,
           send, recv, local):
    me = Place()
    w = Wires(send, recv)
    loads = [pltpu.make_async_copy(grad, gbuf, local.at[0]), pltpu.make_async_copy(mom, mbuf, local.at[1])]
    for load in loads:
        load.start()
    greet([me.zdev(d) for d in range(1, ZS)] + [me.xdev(d) for d in range(1, XS)] + [me.tdev(d) for d in range(1, TP)])

    def load_buffer(s):
        if s == 0:
            for load in loads:
                load.wait()
            gbuf[...] = gbuf[...] + mbuf[...]

    gather_plane(me, w, basis[0], basis[1], bfull0, bslots1, bfull1, load_buffer)

    share = part.shape[2]
    for l in range(LAYERS):
        total = jnp.zeros((part.shape[1] * share, RANK), F32)
        for e in range(XS):
            total = total + dot(gbuf[l, :, me.cols(e)], gathered(bfull0, bfull1, l, e), ((1,), (0,)))
        part[l] = total.reshape(part.shape[1], share, RANK)
    copies = []
    for d in range(1, TP):
        there = lax.rem(me.t + d, TP)
        copies.append(w.go(part.at[lax.rem(there, CS), lax.div(there, CS)], rs.at[d], me.tdev(d)))
    total = part[me.c, me.y]
    for d in range(1, TP):
        copies[d - 1].wait_recv()
        total = total + rs[d]
    q[me.c, me.y] = total
    copies = [w.go(q.at[me.c, me.y], q.at[me.c, me.y], me.tdev(d)) for d in range(1, TP)]
    for copy in copies:
        copy.wait_recv()

    def take(gram):
        for h in range(2):
            a[:, h * HALF : (h + 1) * HALF] = gram[h].reshape(RANK, HALF)

    sums = [sum_gram(me, w, q[me.c].reshape(YS * share, RANK), gs, gfull, zbuf, xbuf)]
    next(sums[0])
    trade = []

    def fill0():
        for e in range(XS):
            cols = dot(gbuf[0, :, me.cols(e)], q[0].reshape(YS * share, RANK), ((0,), (0,)))
            part0[:, e] = cols.reshape(ZS, 16, RANK)

    def fill1(e):
        cols = dot(gbuf[1, :, me.cols(e)], q[1].reshape(YS * share, RANK), ((0,), (0,)))
        tmp[...] = cols.reshape(ZS, 16, RANK)
        for slot, d in enumerate(FAR):
            part1[e, slot] = tmp[me.zat(d)]

    def beside_scatter(s):
        if s in (1, 2, 4, 6):
            next(sums[0], None)
        if s == 6:
            take(gfull)
        for n in {7: (0, 1, 2), 8: (3, 4, 5), 9: (6, 7)}.get(s, ()):
            eliminate(a, w1, n * PANEL)
        if s == 9:
            p1[...] = dot(q[me.c].reshape(YS * share, RANK), w1[...], ((1,), (1,)))
            sums.append(sum_gram(me, w, p1[...], gs2, gfull2, zbuf2, xbuf2))
            next(sums[1])

    def beside_gather(s):
        if s in (0, 1, 3, 5):
            next(sums[1], None)
        if s == 5:
            take(gfull2)
        for n in {5: (0,), 6: (1, 2, 3), 7: (4, 5, 6), 8: (7,)}.get(s, ()):
            eliminate(a, w2, n * PANEL)
        if s == 8:
            wide[me.c] = dot(w2[...], w1[...], ((1,), (0,)))
            trade.append(w.go(wide.at[me.c], wide.at[me.c], me.cdev()))
            p2[me.c] = dot(p1[...], w2[...], ((1,), (1,)))
            trade.append(w.go(p2.at[me.c], p2.at[me.c], me.cdev()))

    own = scatter_plane(me, w, part0, part1, rb0, xb0, rb1, half1, whole1, fill0, fill1, beside_scatter)
    gather_plane(me, w, own[0], own[1], full0, slots1, full1, beside_gather)
    for copy in trade:
        copy.wait_recv()
    for l in range(LAYERS):
        squares = jnp.zeros((1, RANK), F32)
        for e in range(XS):
            block = dot(gathered(full0, full1, l, e), wide[l], ((1,), (1,)))
            if l == 0:
                cols0[:, e] = block.reshape(ZS, 16, RANK)
            else:
                cols1[e] = block.reshape(ZS, 16, RANK)
            squares = squares + jnp.sum(block * block, 0, keepdims=True)
        sq[me.t, l] = jnp.broadcast_to(squares, (8, RANK))
    copies = [w.go(sq.at[me.t], sq.at[me.t], me.tdev(d)) for d in range(1, TP)]
    for l in range(LAYERS):
        for e in range(XS):
            block = gathered(cols0, cols1, l, e)
            new_mom[l, :, me.cols(e)] = gbuf[l, :, me.cols(e)] - (1.0 - keep_rate) * dot3(p2[l], block, 1)
    for copy in copies:
        copy.wait_recv()
    for l in range(LAYERS):
        squares = sq[0, l]
        for t in range(1, TP):
            squares = squares + sq[t, l]
        norm = jnp.sqrt(squares[0:1] + eps)
        new_basis[l] = (cols0[me.z, 0] if l == 0 else cols1[0, me.z]) / norm
        scaled = p2[l] * (math.sqrt(ROWS * COLS / RANK) / norm)
        for e in range(XS):
            update[l, :, me.cols(e)] = dot3(scaled, gathered(cols0, cols1, l, e), 1)
    w.drain()


PANEL = 32


def split3(a):
    high = a.astype(BF16)
    rest = a - high.astype(F32)
    mid = rest.astype(BF16)
    low = (rest - mid.astype(F32)).astype(BF16)
    return high, mid, low


def eliminate(a_ref, w_ref, r0):
    halves = [a_ref[r0 : r0 + PANEL, h * HALF : (h + 1) * HALF] for h in (0, 1)]
    finished = []
    for j0 in range(r0, r0 + PANEL, 8):
        side, start = divmod(j0, HALF)
        height = r0 + PANEL - j0
        lane = lax.broadcasted_iota(jnp.int32, (height, HALF), 1)
        row = lax.broadcasted_iota(jnp.int32, (height, HALF), 0)
        cols = [jnp.broadcast_to(halves[side][:, start + k : start + k + 1], (height, HALF)) for k in range(8)]
        scale = jnp.zeros((8, HALF), F32)
        for k in range(8):
            pivot = cols[k][k : k + 1]
            ratio = jnp.where(row > k, cols[k] * (1.0 / pivot), 0.0)
            scale = jnp.where(row[:8] == k, lax.rsqrt(pivot), scale)
            for n in range(k + 1, 8):
                cols[n] = cols[n] - ratio * cols[n][k : k + 1]
            for h in (0, 1):
                kept, spread = halves[h], halves[h][k : k + 1]
                if h == side:
                    spread = jnp.where(lane[0:1] == start + k, 1.0, spread)
                    kept = jnp.where((lane == start + k) & (row >= k), jnp.where(row == k, 1.0, 0.0), kept)
                halves[h] = kept - ratio * spread
        finished.append([half[:8] * scale for half in halves])
        halves = [half[8:] for half in halves] if height > 8 else None
    whole = jnp.concatenate([jnp.concatenate(rows, 1) for rows in finished], 0)
    lanes = lax.broadcasted_iota(jnp.int32, (PANEL, RANK), 1)
    rows = lax.broadcasted_iota(jnp.int32, (PANEL, RANK), 0) + r0
    w_ref[r0 : r0 + PANEL, :] = jnp.where(lanes <= rows, whole, 0.0)
    rest = r0 + PANEL
    if rest < RANK:
        right = jnp.where((lanes > rows) & (lanes < rest), 0.0, whole)
        h, m, l = split3(whole)
        hr, mr, lr = split3(right)
        left = jnp.concatenate([h, h, m, h, l, m], 0)
        base = rest // HALF * HALF
        change = lax.dot_general(
            left[:, base:], jnp.concatenate([hr, mr, hr, lr, hr, mr], 0),
            (((0,), (0,)), ((), ())), preferred_element_type=F32)
        wide = lax.broadcasted_iota(jnp.int32, (RANK - rest, RANK), 1)
        old = jnp.where((wide >= r0) & (wide < rest), 0.0, a_ref[rest:, :])
        a_ref[rest:, :] = old - change[rest - base :, :]


def vmem(*shape):
    return pltpu.VMEM(shape, F32)


V = pl.BlockSpec(memory_space=pltpu.VMEM)
ANY = pl.BlockSpec(memory_space=pl.ANY)
COPIES = 288


def per_device(gradient, momentum, basis):
    rows, cols = gradient.shape[1:]
    share = basis.shape[1]
    whole = jax.ShapeDtypeStruct((LAYERS, rows, cols), F32)
    plane = [vmem(ZS, XS, share, RANK), vmem(XS, ZS, share, RANK), vmem(XS, ZS, share, RANK)]
    sums = [vmem(2, RANK // 8, 8, HALF), vmem(2, RANK // 8, 8, HALF), vmem(ZS, 8, HALF), vmem(XS, 8, HALF)]
    return pl.pallas_call(
        kernel,
        out_shape=(whole, jax.ShapeDtypeStruct((LAYERS, share, RANK), F32), whole),
        in_specs=[ANY, ANY, V],
        out_specs=(V, V, V),
        scratch_shapes=[
            vmem(LAYERS, rows, cols), vmem(LAYERS, rows, cols), *plane,
            vmem(LAYERS, YS, rows // YS, RANK), vmem(TP, rows // YS, RANK), vmem(LAYERS, YS, rows // YS, RANK),
            vmem(rows, RANK), vmem(LAYERS, rows, RANK),
            vmem(RANK, RANK), vmem(RANK, RANK), vmem(RANK, RANK), vmem(LAYERS, RANK, RANK),
            *sums, *sums,
            vmem(ZS, XS, share, RANK), vmem(XS, ZS, share, RANK), vmem(ZS, share, RANK), *plane,
            vmem(2, 8, XS, share, RANK), vmem(XS, share, RANK), vmem(2, 8, share, RANK),
            vmem(ZS, share, RANK), vmem(2, ZS, share, RANK),
            vmem(ZS, XS, share, RANK), vmem(XS, ZS, share, RANK), vmem(TP, LAYERS, 8, RANK),
            pltpu.SemaphoreType.DMA((COPIES,)), pltpu.SemaphoreType.DMA((COPIES,)), pltpu.SemaphoreType.DMA((2,)),
        ],
        compiler_params=pltpu.CompilerParams(
            collective_id=0, has_side_effects=True, vmem_limit_bytes=60 * 2**20),
        name="step",
    )(gradient, momentum, basis)


def solution(mesh):
    return jax.shard_map(
        per_device,
        mesh=mesh,
        in_specs=(P(None, "fsdp", "tp"), P(None, "fsdp", "tp"), P(None, ("tp", "fsdp"), None)),
        out_specs=(P(None, "fsdp", "tp"), P(None, ("tp", "fsdp"), None), P(None, "fsdp", "tp")),
        check_vma=False,
    )
```

```python
import math

import jax
import jax.numpy as jnp
from jax import lax
from jax.experimental import pallas as pl
from jax.experimental.pallas import tpu as pltpu
from jax.sharding import PartitionSpec as P

ROWS = 8192
COLS = 8192
RANK = 256
LAYERS = 2
XS, ZS, YS, CS = 4, 16, 4, 2
TP = YS * CS
MESH = pl.DeviceIdType.MESH
HIGHEST = lax.Precision.HIGHEST
F32 = jnp.float32
BF16 = jnp.bfloat16
HALF = RANK // 2

keep_rate = 0.95
eps = 1e-06


def dot(a, b, dims):
    return lax.dot_general(a, b, (dims, ((), ())), precision=HIGHEST, preferred_element_type=F32)


def split2(a):
    high = a.astype(BF16)
    return high, (a - high.astype(F32)).astype(BF16)


def dot3(a, b, axis):
    ah, al = split2(a)
    bh, bl = split2(b)
    return lax.dot_general(
        jnp.concatenate([ah, ah, al], axis), jnp.concatenate([bh, bl, bh], axis),
        (((axis,), (axis,)), ((), ())), preferred_element_type=F32)


class Place:
    def __init__(self):
        self.f = lax.axis_index("fsdp")
        self.t = lax.axis_index("tp")
        self.x = lax.div(self.f, ZS)
        self.z = lax.rem(self.f, ZS)
        self.y = lax.div(self.t, CS)
        self.c = lax.rem(self.t, CS)

    def zat(self, d):
        return lax.rem(self.z + (ZS + d), ZS)

    def xat(self, d):
        return lax.rem(self.x + (XS + d), XS)

    def yat(self, d):
        return lax.rem(self.y + (YS + d), YS)

    def cols(self, e):
        return pl.ds(pl.multiple_of(self.xat(e) * 256, 256), 256)

    def zdev(self, d):
        return (self.x * ZS + self.zat(d), self.t)

    def xdev(self, d):
        return (self.xat(d) * ZS + self.z, self.t)

    def tdev(self, d):
        return (self.f, lax.rem(self.t + (TP + d), TP))

    def ydev(self, d):
        return (self.f, self.yat(d) * CS + self.c)

    def cdev(self):
        return (self.f, self.y * CS + (1 - self.c))


class Wires:
    def __init__(self, send, recv):
        self.send, self.recv, self.used = send, recv, 0
        self.sent = []

    def go(self, src, dst, device):
        i = self.used
        self.used += 1
        copy = pltpu.make_async_remote_copy(
            src_ref=src, dst_ref=dst, send_sem=self.send.at[i], recv_sem=self.recv.at[i],
            device_id=device, device_id_type=MESH,
        )
        copy.start()
        self.sent.append(copy)
        return copy

    def drain(self, keep=0):
        while len(self.sent) > keep:
            self.sent.pop(0).wait_send()


def gathered(full0, full1, l, e):
    block = full0[:, e] if l == 0 else full1[e]
    return block.reshape(256, RANK)


def greet(devices):
    barrier = pltpu.get_barrier_semaphore()
    for device in devices:
        pl.semaphore_signal(barrier, inc=1, device_id=device, device_id_type=MESH)
    pl.semaphore_wait(barrier, len(devices))


WAYS = ((1, 8), (-1, 7))


def near(way, d):
    return 0 if d == 0 else 2 * d - 1 if way == 1 else 2 * d


def offset(slot):
    return 0 if slot == 0 else -((slot + 1) // 2) if slot % 2 else slot // 2


GROUPS = ((0, 5), (5, 9), (9, 13), (13, 16))


def gather_plane(me, w, own0, own1, full0, slots1, full1, beside):
    full0[me.z, 0] = own0
    slots1[0, 0] = own1
    full1[0, me.z] = own1
    xa = {e: w.go(full0.at[me.z, 0], full0.at[me.z, (-e) % XS], me.xdev(e)) for e in (3, 1, 2)}
    ring, wide, ahead = {}, {}, {}

    def hop_b(s):
        for way, last in WAYS:
            if 0 < s <= last:
                ring["b", way, s - 1].wait_recv()
            if s < last:
                ring["b", way, s] = w.go(
                    slots1.at[0, near(way, s)], slots1.at[0, near(way, s + 1)], me.zdev(way))

    def hop_a(s):
        for half in (0, 1):
            pair = pl.ds(2 * half, 2)
            for way, last in WAYS:
                if s == 0 and way == 1:
                    for e in ((3,), (1, 2))[half]:
                        xa[e].wait_recv()
                if 0 < s <= last:
                    ring["a", way, s - 1, half].wait_recv()
                if s < last:
                    block = full0.at[me.zat(-way * s), pair]
                    ring["a", way, s, half] = w.go(block, block, me.zdev(way))

    def spread(g):
        lo, hi = GROUPS[g]
        group = slots1.at[0, pl.ds(lo, hi - lo)]
        wide[g] = [w.go(group, slots1.at[(-e) % XS, pl.ds(lo, hi - lo)], me.xdev(e)) for e in (1, -1)]
        for i in range(lo, hi):
            full1[0, me.zat(offset(i))] = slots1[0, i]

    def forward(g):
        lo, hi = GROUPS[g]
        mid = (lo + hi) // 2
        ahead[g] = []
        for n, (a, b, e) in enumerate(((lo, mid, 1), (mid, hi, -1))):
            wide[g][n].wait_recv()
            ahead[g].append(
                w.go(slots1.at[(-e) % XS, pl.ds(a, b - a)], slots1.at[2, pl.ds(a, b - a)], me.xdev(e)))
        for i in range(lo, hi):
            for e in (1, 3):
                full1[e, me.zat(offset(i))] = slots1[e, i]

    for s in range(9):
        hop_b(s)
        if s in (2, 4, 6, 8):
            spread(s // 2 - 1)
        hop_a(s)
        if s in (4, 6, 8):
            forward(s // 2 - 2)
        beside(s)
        w.drain(64)
    forward(3)
    beside(9)
    for g in range(4):
        for copy in ahead[g]:
            copy.wait_recv()
        for i in range(*GROUPS[g]):
            full1[2, me.zat(offset(i))] = slots1[2, i]


FAR = [8] + [d for r in range(7, 0, -1) for d in (r, -r)] + [0]
FAR_GROUPS = ((0, 3), (3, 7), (7, 11), (11, 16))


def scatter_plane(me, w, part0, part1, rb0, xb0, rb1, half1, whole1, fill0, fill1, beside):
    first, second, ring = {}, {}, {}

    def begin(g):
        lo, hi = FAR_GROUPS[g]
        mid = (lo + hi) // 2
        first[g] = [
            w.go(part1.at[2, pl.ds(a, b - a)], half1.at[pl.ds(a, b - a)], me.xdev(e))
            for a, b, e in ((lo, mid, 1), (mid, hi, -1))
        ]

    def pass_on(g):
        lo, hi = FAR_GROUPS[g]
        mid = (lo + hi) // 2
        second[g] = []
        for n, (a, b, e) in enumerate(((lo, mid, 1), (mid, hi, -1))):
            first[g][n].wait_recv()
            part1[e % XS, a:b] = part1[e % XS, a:b] + half1[a:b]
            second[g].append(
                w.go(part1.at[e % XS, pl.ds(lo, hi - lo)], whole1.at[n, pl.ds(lo, hi - lo)], me.xdev(e)))

    def collect(g):
        lo, hi = FAR_GROUPS[g]
        for copy in second[g]:
            copy.wait_recv()
        part1[0, lo:hi] = part1[0, lo:hi] + whole1[0, lo:hi] + whole1[1, lo:hi]

    def hop_a(s):
        for half in (0, 1):
            lo, hi = 2 * half, 2 * half + 2
            pair = pl.ds(lo, 2)
            for k, (way, last) in enumerate(WAYS):
                if s > last:
                    continue
                there = me.zat(way * (last - s))
                if s == 0:
                    ring["a", way, 0, half] = w.go(part0.at[there, pair], rb0.at[k, 0, pair], me.zdev(way))
                    continue
                ring["a", way, s - 1, half].wait_recv()
                if s < last:
                    rb0[k, s - 1, lo:hi] = rb0[k, s - 1, lo:hi] + part0[there, lo:hi]
                    ring["a", way, s, half] = w.go(rb0.at[k, s - 1, pair], rb0.at[k, s, pair], me.zdev(way))

    def hop_b(s):
        for k, (way, last) in enumerate(WAYS):
            if s > last:
                continue
            slot = FAR.index(way * (last - s))
            if s == 0:
                ring["b", way, 0] = w.go(part1.at[0, slot], rb1.at[k, 0], me.zdev(way))
                continue
            ring["b", way, s - 1].wait_recv()
            if s < last:
                rb1[k, s - 1] = rb1[k, s - 1] + part1[0, slot]
                ring["b", way, s] = w.go(rb1.at[k, s - 1], rb1.at[k, s], me.zdev(way))

    fill1(2)
    for g in range(4):
        begin(g)
    fill0()
    copies = []
    for s in range(11):
        if s <= 8:
            hop_a(s)
        if s == 0:
            fill1(1)
            fill1(3)
        if s == 1:
            fill1(0)
        if s == 8:
            rb0[0, 7] = rb0[0, 7] + part0[me.z] + rb0[1, 6]
            copies = [w.go(rb0.at[0, 7, e], xb0.at[e], me.xdev(e)) for e in (2, 1, 3)]
        if s in (0, 2, 4, 6):
            pass_on(s // 2)
        if s in (1, 3, 5, 7):
            collect(s // 2)
        if s >= 2:
            hop_b(s - 2)
        beside(s)
        w.drain(64)
    for copy in copies:
        copy.wait_recv()
    return rb0[0, 7, 0] + xb0[1] + xb0[2] + xb0[3], part1[0, 15] + rb1[0, 7] + rb1[1, 6]


QUARTERS = ((0, 0), (0, 1), (1, 1), (1, 0))


def sum_gram(me, w, product, gs, gfull, zbuf, xbuf):
    gram = dot(product, product, ((0,), (0,)))
    for n, (r, h) in enumerate(QUARTERS):
        gs[n] = gram[r * HALF : (r + 1) * HALF, h * HALF : (h + 1) * HALF].reshape(HALF // 8, 8, HALF)

    def tile(ref, z):
        return ref.at[lax.div(z, 4), me.y * 4 + lax.rem(z, 4)]

    far = [8] + [d for r in range(7, 0, -1) for d in (r, ZS - r)]
    copies = [w.go(tile(gs, me.zat(d)), zbuf.at[d], me.zdev(d)) for d in far]
    yield
    total = gs[lax.div(me.z, 4), me.y * 4 + lax.rem(me.z, 4)]
    for d, copy in reversed(list(zip(far, copies))):
        copy.wait_recv()
        total = total + zbuf[d]
    xbuf[me.x] = total
    copies = [w.go(xbuf.at[me.x], xbuf.at[me.x], me.xdev(d)) for d in (2, 1, 3)]
    yield
    for copy in copies:
        copy.wait_recv()
    gfull[lax.div(me.z, 4), me.y * 4 + lax.rem(me.z, 4)] = xbuf[0] + xbuf[1] + xbuf[2] + xbuf[3]
    copies = [w.go(tile(gfull, me.z), tile(gfull, me.z), me.zdev(d)) for d in far]
    yield
    for copy in reversed(copies):
        copy.wait_recv()
    mine = gfull.at[pl.ds(0, 3), pl.ds(me.y * 4, 4)]
    copies = [w.go(mine, mine, me.ydev(d)) for d in (2, 1, 3)]
    yield
    for copy in copies:
        copy.wait_recv()


def kernel(grad, mom, basis, new_mom, new_basis, update,
           gbuf, mbuf, bfull0, bslots1, bfull1, part, rs, q, p1, p2, a, w1, w2, wide,
           gs, gfull, zbuf, xbuf, gs2, gfull2, zbuf2, xbuf2,
           part0, part1, tmp, full0, slots1, full1, rb0, xb0, rb1, half1, whole1, cols0, cols1, sq, out,
           send, recv, local):
    me = Place()
    w = Wires(send, recv)
    loads = [pltpu.make_async_copy(grad, gbuf, local.at[0]), pltpu.make_async_copy(mom, mbuf, local.at[1])]
    for load in loads:
        load.start()
    greet([me.zdev(d) for d in range(1, ZS)] + [me.xdev(d) for d in range(1, XS)] + [me.tdev(d) for d in range(1, TP)])

    share = part.shape[2]

    def multiply(l):
        total = jnp.zeros((part.shape[1] * share, RANK), F32)
        for e in range(XS):
            total = total + dot(gbuf[l, :, me.cols(e)], gathered(bfull0, bfull1, l, e), ((1,), (0,)))
        part[l] = total.reshape(part.shape[1], share, RANK)

    def beside_basis(s):
        if s == 0:
            for load in loads:
                load.wait()
            gbuf[...] = gbuf[...] + mbuf[...]
        if s == 9:
            multiply(0)

    gather_plane(me, w, basis[0], basis[1], bfull0, bslots1, bfull1, beside_basis)
    multiply(1)
    copies = []
    away = (4, 3, 5, 2, 6, 1, 7)
    for d in away:
        there = lax.rem(me.t + d, TP)
        copies.append(w.go(part.at[lax.rem(there, CS), lax.div(there, CS)], rs.at[d], me.tdev(d)))
    total = part[me.c, me.y]
    for d, copy in zip(away, copies):
        copy.wait_recv()
        total = total + rs[d]
    q[me.c, me.y] = total
    copies = [w.go(q.at[me.c, me.y], q.at[me.c, me.y], me.ydev(d)) for d in (2, 1, 3)]
    for copy in copies:
        copy.wait_recv()
    swap = w.go(q.at[me.c], q.at[me.c], me.cdev())

    def take(gram):
        for n, (r, h) in enumerate(QUARTERS):
            quarter = gram[n].reshape(HALF, HALF) if n < 3 else jnp.zeros((HALF, HALF), F32)
            a[r * HALF : (r + 1) * HALF, h * HALF : (h + 1) * HALF] = quarter

    sums = [sum_gram(me, w, q[me.c].reshape(YS * share, RANK), gs, gfull, zbuf, xbuf)]
    next(sums[0])
    swap.wait_recv()
    trade = []

    def fill0():
        for e in range(XS):
            cols = dot(gbuf[0, :, me.cols(e)], q[0].reshape(YS * share, RANK), ((0,), (0,)))
            part0[:, e] = cols.reshape(ZS, 16, RANK)

    def fill1(e):
        cols = dot(gbuf[1, :, me.cols(e)], q[1].reshape(YS * share, RANK), ((0,), (0,)))
        tmp[...] = cols.reshape(ZS, 16, RANK)
        for slot, d in enumerate(FAR):
            part1[e, slot] = tmp[me.zat(d)]

    def beside_scatter(s):
        if s in (1, 2, 4, 6):
            next(sums[0], None)
        if s == 6:
            take(gfull)
        for n in {7: (0, 1, 2), 8: (3, 4, 5), 9: (6, 7)}.get(s, ()):
            eliminate(a, w1, n * PANEL)
        if s == 9:
            p1[...] = dot(q[me.c].reshape(YS * share, RANK), w1[...], ((1,), (1,)))
            sums.append(sum_gram(me, w, p1[...], gs2, gfull2, zbuf2, xbuf2))
            next(sums[1])

    def beside_gather(s):
        if s in (0, 1, 3, 5):
            next(sums[1], None)
        if s == 5:
            take(gfull2)
        for n in {5: (0,), 6: (1, 2, 3), 7: (4, 5, 6), 8: (7,)}.get(s, ()):
            eliminate(a, w2, n * PANEL)
        if s == 9:
            for copy in trade:
                copy.wait_recv()
            finish(0)
        if s == 8:
            wide[me.c] = dot(w2[...], w1[...], ((1,), (0,)))
            trade.append(w.go(wide.at[me.c], wide.at[me.c], me.cdev()))
            p2[me.c] = dot(p1[...], w2[...], ((1,), (1,)))
            trade.append(w.go(p2.at[me.c], p2.at[me.c], me.cdev()))

    def finish(l):
        squares = jnp.zeros((1, RANK), F32)
        for e in range(XS):
            block = dot(gathered(full0, full1, l, e), wide[l], ((1,), (1,)))
            if l == 0:
                cols0[:, e] = block.reshape(ZS, 16, RANK)
            else:
                cols1[e] = block.reshape(ZS, 16, RANK)
            squares = squares + jnp.sum(block * block, 0, keepdims=True)
        sq[me.t, l] = jnp.broadcast_to(squares, (8, RANK))

    own = scatter_plane(me, w, part0, part1, rb0, xb0, rb1, half1, whole1, fill0, fill1, beside_scatter)
    gather_plane(me, w, own[0], own[1], full0, slots1, full1, beside_gather)
    finish(1)
    stores = []
    copies = [w.go(sq.at[me.t], sq.at[me.t], me.tdev(d)) for d in range(1, TP)]
    for l in range(LAYERS):
        for e in range(XS):
            block = gathered(cols0, cols1, l, e)
            mbuf[l, :, me.cols(e)] = gbuf[l, :, me.cols(e)] - (1.0 - keep_rate) * dot3(p2[l], block, 1)
        stores.append(pltpu.make_async_copy(mbuf.at[l], new_mom.at[l], local.at[2 + l]))
        stores[-1].start()
    for copy in copies:
        copy.wait_recv()
    for l in range(LAYERS):
        squares = sq[0, l]
        for t in range(1, TP):
            squares = squares + sq[t, l]
        norm = jnp.sqrt(squares[0:1] + eps)
        new_basis[l] = (cols0[me.z, 0] if l == 0 else cols1[0, me.z]) / norm
        scaled = p2[l] * (math.sqrt(ROWS * COLS / RANK) / norm)
        for e in range(XS):
            out[l, :, me.cols(e)] = dot3(scaled, gathered(cols0, cols1, l, e), 1)
        stores.append(pltpu.make_async_copy(out.at[l], update.at[l], local.at[4 + l]))
        stores[-1].start()
    w.drain()
    for store in stores:
        store.wait()


PANEL = 32


def split3(a):
    high = a.astype(BF16)
    rest = a - high.astype(F32)
    mid = rest.astype(BF16)
    low = (rest - mid.astype(F32)).astype(BF16)
    return high, mid, low


def eliminate(a_ref, w_ref, r0):
    halves = [a_ref[r0 : r0 + PANEL, h * HALF : (h + 1) * HALF] for h in (0, 1)]
    finished = []
    for j0 in range(r0, r0 + PANEL, 8):
        side, start = divmod(j0, HALF)
        height = r0 + PANEL - j0
        lane = lax.broadcasted_iota(jnp.int32, (height, HALF), 1)
        row = lax.broadcasted_iota(jnp.int32, (height, HALF), 0)
        cols = [jnp.broadcast_to(halves[side][:, start + k : start + k + 1], (height, HALF)) for k in range(8)]
        scale = jnp.zeros((8, HALF), F32)
        for k in range(8):
            pivot = cols[k][k : k + 1]
            ratio = jnp.where(row > k, cols[k] * (1.0 / pivot), 0.0)
            scale = jnp.where(row[:8] == k, lax.rsqrt(pivot), scale)
            for n in range(k + 1, 8):
                cols[n] = cols[n] - ratio * cols[n][k : k + 1]
            for h in (0, 1):
                kept, spread = halves[h], halves[h][k : k + 1]
                if h == side:
                    spread = jnp.where(lane[0:1] == start + k, 1.0, spread)
                    kept = jnp.where((lane == start + k) & (row >= k), jnp.where(row == k, 1.0, 0.0), kept)
                halves[h] = kept - ratio * spread
        finished.append([half[:8] * scale for half in halves])
        halves = [half[8:] for half in halves] if height > 8 else None
    whole = jnp.concatenate([jnp.concatenate(rows, 1) for rows in finished], 0)
    lanes = lax.broadcasted_iota(jnp.int32, (PANEL, RANK), 1)
    rows = lax.broadcasted_iota(jnp.int32, (PANEL, RANK), 0) + r0
    w_ref[r0 : r0 + PANEL, :] = jnp.where(lanes <= rows, whole, 0.0)
    rest = r0 + PANEL
    if rest < RANK:
        right = jnp.where((lanes > rows) & (lanes < rest), 0.0, whole)
        h, m, l = split3(whole)
        hr, mr, lr = split3(right)
        left = jnp.concatenate([h, h, m, h, l, m], 0)
        base = rest // HALF * HALF
        change = lax.dot_general(
            left[:, base:], jnp.concatenate([hr, mr, hr, lr, hr, mr], 0),
            (((0,), (0,)), ((), ())), preferred_element_type=F32)
        wide = lax.broadcasted_iota(jnp.int32, (RANK - rest, RANK), 1)
        old = jnp.where((wide >= r0) & (wide < rest), 0.0, a_ref[rest:, :])
        a_ref[rest:, :] = old - change[rest - base :, :]


def hand_over(a, b, c, a_out, b_out, c_out, sems):
    copies = [
        pltpu.make_async_copy(source.at[l], target.at[l], sems.at[n, l])
        for n, (source, target) in enumerate(((a, a_out), (b, b_out), (c, c_out))) for l in range(LAYERS)
    ]
    for copy in copies:
        copy.start()
    for copy in copies:
        copy.wait()


def vmem(*shape):
    return pltpu.VMEM(shape, F32)


V = pl.BlockSpec(memory_space=pltpu.VMEM)
ANY = pl.BlockSpec(memory_space=pl.ANY)
COPIES = 288


def per_device(gradient, momentum, basis):
    rows, cols = gradient.shape[1:]
    share = basis.shape[1]
    whole = jax.ShapeDtypeStruct((LAYERS, rows, cols), F32)
    plane = [vmem(ZS, XS, share, RANK), vmem(XS, ZS, share, RANK), vmem(XS, ZS, share, RANK)]
    sums = [vmem(4, HALF // 8, 8, HALF), vmem(4, HALF // 8, 8, HALF), vmem(ZS, 8, HALF), vmem(XS, 8, HALF)]
    shapes = (whole, jax.ShapeDtypeStruct((LAYERS, share, RANK), F32), whole)
    results = pl.pallas_call(
        kernel,
        out_shape=shapes,
        in_specs=[ANY, ANY, V],
        out_specs=(ANY, V, ANY),
        scratch_shapes=[
            vmem(LAYERS, rows, cols), vmem(LAYERS, rows, cols), *plane,
            vmem(LAYERS, YS, rows // YS, RANK), vmem(TP, rows // YS, RANK), vmem(LAYERS, YS, rows // YS, RANK),
            vmem(rows, RANK), vmem(LAYERS, rows, RANK),
            vmem(RANK, RANK), vmem(RANK, RANK), vmem(RANK, RANK), vmem(LAYERS, RANK, RANK),
            *sums, *sums,
            vmem(ZS, XS, share, RANK), vmem(XS, ZS, share, RANK), vmem(ZS, share, RANK), *plane,
            vmem(2, 8, XS, share, RANK), vmem(XS, share, RANK), vmem(2, 8, share, RANK),
            vmem(ZS, share, RANK), vmem(2, ZS, share, RANK),
            vmem(ZS, XS, share, RANK), vmem(XS, ZS, share, RANK), vmem(TP, LAYERS, 8, RANK), vmem(LAYERS, rows, cols),
            pltpu.SemaphoreType.DMA((COPIES,)), pltpu.SemaphoreType.DMA((COPIES,)), pltpu.SemaphoreType.DMA((6,)),
        ],
        compiler_params=pltpu.CompilerParams(
            collective_id=0, has_side_effects=True, vmem_limit_bytes=60 * 2**20),
        name="step",
    )(gradient, momentum, basis)
    return pl.pallas_call(
        hand_over,
        out_shape=shapes,
        in_specs=[ANY] * 3,
        out_specs=(ANY,) * 3,
        scratch_shapes=[pltpu.SemaphoreType.DMA((3, LAYERS))],
        compiler_params=pltpu.CompilerParams(vmem_limit_bytes=60 * 2**20),
        name="hand_over",
    )(*results)


def solution(mesh):
    return jax.shard_map(
        per_device,
        mesh=mesh,
        in_specs=(P(None, "fsdp", "tp"), P(None, "fsdp", "tp"), P(None, ("tp", "fsdp"), None)),
        out_specs=(P(None, "fsdp", "tp"), P(None, ("tp", "fsdp"), None), P(None, "fsdp", "tp")),
        check_vma=False,
    )
```

```python
import math

import jax
import jax.numpy as jnp
from jax import lax
from jax.experimental import pallas as pl
from jax.experimental.pallas import tpu as pltpu
from jax.sharding import PartitionSpec as P

ROWS = 8192
COLS = 8192
RANK = 256
LAYERS = 2
XS, ZS, YS, CS = 4, 16, 4, 2
TP = YS * CS
MESH = pl.DeviceIdType.MESH
HIGHEST = lax.Precision.HIGHEST
F32 = jnp.float32
BF16 = jnp.bfloat16
HALF = RANK // 2

keep_rate = 0.95
eps = 1e-06


def dot(a, b, dims):
    return lax.dot_general(a, b, (dims, ((), ())), precision=HIGHEST, preferred_element_type=F32)


def split2(a):
    high = a.astype(BF16)
    return high, (a - high.astype(F32)).astype(BF16)


def dot3(a, b, axis):
    ah, al = split2(a)
    bh, bl = split2(b)
    return lax.dot_general(
        jnp.concatenate([ah, ah, al], axis), jnp.concatenate([bh, bl, bh], axis),
        (((axis,), (axis,)), ((), ())), preferred_element_type=F32)


class Place:
    def __init__(self):
        self.f = lax.axis_index("fsdp")
        self.t = lax.axis_index("tp")
        self.x = lax.div(self.f, ZS)
        self.z = lax.rem(self.f, ZS)
        self.y = lax.div(self.t, CS)
        self.c = lax.rem(self.t, CS)

    def zat(self, d):
        return lax.rem(self.z + (ZS + d), ZS)

    def xat(self, d):
        return lax.rem(self.x + (XS + d), XS)

    def yat(self, d):
        return lax.rem(self.y + (YS + d), YS)

    def cols(self, e):
        return pl.ds(pl.multiple_of(self.xat(e) * 256, 256), 256)

    def zdev(self, d):
        return (self.x * ZS + self.zat(d), self.t)

    def xdev(self, d):
        return (self.xat(d) * ZS + self.z, self.t)

    def tdev(self, d):
        return (self.f, lax.rem(self.t + (TP + d), TP))

    def ydev(self, d):
        return (self.f, self.yat(d) * CS + self.c)

    def cdev(self):
        return (self.f, self.y * CS + (1 - self.c))


class Wires:
    def __init__(self, send, recv):
        self.send, self.recv, self.used = send, recv, 0
        self.sent = []

    def go(self, src, dst, device):
        i = self.used
        self.used += 1
        copy = pltpu.make_async_remote_copy(
            src_ref=src, dst_ref=dst, send_sem=self.send.at[i], recv_sem=self.recv.at[i],
            device_id=device, device_id_type=MESH,
        )
        copy.start()
        self.sent.append(copy)
        return copy

    def drain(self, keep=0):
        while len(self.sent) > keep:
            self.sent.pop(0).wait_send()


def gathered(full0, full1, l, e):
    block = full0[:, e] if l == 0 else full1[e]
    return block.reshape(256, RANK)


def greet(devices):
    barrier = pltpu.get_barrier_semaphore()
    for device in devices:
        pl.semaphore_signal(barrier, inc=1, device_id=device, device_id_type=MESH)
    pl.semaphore_wait(barrier, len(devices))


WAYS = ((1, 8), (-1, 7))


def near(way, d):
    return 0 if d == 0 else 2 * d - 1 if way == 1 else 2 * d


STREAMS = {0: ((1, 2), (-1, 2)), -5: ((1, 3), (-1, 2)), 5: ((1, 2), (-1, 2))}


def slot_of(c, way, d):
    return 15 if d == 3 else {0: 0, -5: 5, 5: 10}[c] + near(way, d)


OFFSETS = {slot_of(c, way, d): c - way * d for c in STREAMS for way, hops in STREAMS[c] for d in range(hops + 1)}
GROUPS = ((0, 5), (5, 10), (10, 16))


def gather_plane(me, w, own0, own1, full0, slots1, full1, beside):
    full0[me.z, 0] = own0
    slots1[0, 0] = own1
    full1[0, me.z] = own1
    xa = {e: w.go(full0.at[me.z, 0], full0.at[me.z, (-e) % XS], me.xdev(e)) for e in (3, 1, 2)}
    ring, wide, ahead = {}, {}, {}
    for c in (-5, 5):
        ring["b", c] = w.go(slots1.at[0, 0], slots1.at[0, slot_of(c, 1, 0)], me.zdev(-c))

    def hop_b(s):
        for c, ways in STREAMS.items():
            i = s if c == 0 else s - 2
            if i == 0 and c != 0:
                ring["b", c].wait_recv()
            for way, last in ways:
                if 0 < i <= last:
                    ring["b", c, way, i - 1].wait_recv()
                if 0 <= i < last:
                    ring["b", c, way, i] = w.go(
                        slots1.at[0, slot_of(c, way, i)], slots1.at[0, slot_of(c, way, i + 1)], me.zdev(way))

    def hop_a(s):
        for half in (0, 1):
            pair = pl.ds(2 * half, 2)
            if s == 0:
                for e in ((3,), (1, 2))[half]:
                    xa[e].wait_recv()
                block = full0.at[me.z, pair]
                for c in (-5, 5):
                    ring["a", c, half] = w.go(block, block, me.zdev(-c))
            for c, ways in STREAMS.items():
                i = s if c == 0 else s - 3
                if i == 0 and c != 0:
                    ring["a", c, half].wait_recv()
                for way, last in ways:
                    if 0 < i <= last:
                        ring["a", c, way, i - 1, half].wait_recv()
                    if 0 <= i < last:
                        block = full0.at[me.zat(c - way * i), pair]
                        ring["a", c, way, i, half] = w.go(block, block, me.zdev(way))

    def spread(g):
        lo, hi = GROUPS[g]
        group = slots1.at[0, pl.ds(lo, hi - lo)]
        wide[g] = [w.go(group, slots1.at[(-e) % XS, pl.ds(lo, hi - lo)], me.xdev(e)) for e in (1, -1)]
        for i in range(lo, hi):
            full1[0, me.zat(OFFSETS[i])] = slots1[0, i]

    def forward(g):
        lo, hi = GROUPS[g]
        mid = (lo + hi) // 2
        ahead[g] = []
        for n, (a, b, e) in enumerate(((lo, mid, 1), (mid, hi, -1))):
            wide[g][n].wait_recv()
            ahead[g].append(
                w.go(slots1.at[(-e) % XS, pl.ds(a, b - a)], slots1.at[2, pl.ds(a, b - a)], me.xdev(e)))
        for i in range(lo, hi):
            for e in (1, 3):
                full1[e, me.zat(OFFSETS[i])] = slots1[e, i]

    for s in range(7):
        hop_b(s)
        if s in (2, 4, 5):
            spread((2, 4, 5).index(s))
        hop_a(s)
        if s in (4, 6):
            forward(s // 2 - 2)
        beside(s)
        w.drain(64)
    forward(2)
    beside(9)
    for g in range(3):
        for copy in ahead[g]:
            copy.wait_recv()
        for i in range(*GROUPS[g]):
            full1[2, me.zat(OFFSETS[i])] = slots1[2, i]


FAR = [8] + [d for r in range(7, 0, -1) for d in (r, -r)] + [0]
FAR_GROUPS = ((0, 3), (3, 7), (7, 11), (11, 16))


def scatter_plane(me, w, part0, part1, rb0, xb0, rb1, half1, whole1, fill0, fill1, beside):
    first, second, ring = {}, {}, {}

    def begin(g):
        lo, hi = FAR_GROUPS[g]
        mid = (lo + hi) // 2
        first[g] = [
            w.go(part1.at[2, pl.ds(a, b - a)], half1.at[pl.ds(a, b - a)], me.xdev(e))
            for a, b, e in ((lo, mid, 1), (mid, hi, -1))
        ]

    def pass_on(g):
        lo, hi = FAR_GROUPS[g]
        mid = (lo + hi) // 2
        second[g] = []
        for n, (a, b, e) in enumerate(((lo, mid, 1), (mid, hi, -1))):
            first[g][n].wait_recv()
            part1[e % XS, a:b] = part1[e % XS, a:b] + half1[a:b]
            second[g].append(
                w.go(part1.at[e % XS, pl.ds(lo, hi - lo)], whole1.at[n, pl.ds(lo, hi - lo)], me.xdev(e)))

    def collect(g):
        lo, hi = FAR_GROUPS[g]
        for copy in second[g]:
            copy.wait_recv()
        part1[0, lo:hi] = part1[0, lo:hi] + whole1[0, lo:hi] + whole1[1, lo:hi]

    def hop_a(s):
        for half in (0, 1):
            lo, hi = 2 * half, 2 * half + 2
            pair = pl.ds(lo, 2)
            for k, (way, last) in enumerate(WAYS):
                if s > last:
                    continue
                there = me.zat(way * (last - s))
                if s == 0:
                    ring["a", way, 0, half] = w.go(part0.at[there, pair], rb0.at[k, 0, pair], me.zdev(way))
                    continue
                ring["a", way, s - 1, half].wait_recv()
                if s < last:
                    rb0[k, s - 1, lo:hi] = rb0[k, s - 1, lo:hi] + part0[there, lo:hi]
                    ring["a", way, s, half] = w.go(rb0.at[k, s - 1, pair], rb0.at[k, s, pair], me.zdev(way))

    def hop_b(s):
        for k, (way, last) in enumerate(WAYS):
            if s > last:
                continue
            slot = FAR.index(way * (last - s))
            if s == 0:
                ring["b", way, 0] = w.go(part1.at[0, slot], rb1.at[k, 0], me.zdev(way))
                continue
            ring["b", way, s - 1].wait_recv()
            if s < last:
                rb1[k, s - 1] = rb1[k, s - 1] + part1[0, slot]
                ring["b", way, s] = w.go(rb1.at[k, s - 1], rb1.at[k, s], me.zdev(way))

    fill1(2)
    for g in range(4):
        begin(g)
    fill0()
    copies = []
    for s in range(11):
        if s <= 8:
            hop_a(s)
        if s == 0:
            fill1(1)
            fill1(3)
        if s == 1:
            fill1(0)
        if s == 8:
            rb0[0, 7] = rb0[0, 7] + part0[me.z] + rb0[1, 6]
            copies = [w.go(rb0.at[0, 7, e], xb0.at[e], me.xdev(e)) for e in (2, 1, 3)]
        if s in (0, 2, 4, 6):
            pass_on(s // 2)
        if s in (1, 3, 5, 7):
            collect(s // 2)
        if s >= 2:
            hop_b(s - 2)
        beside(s)
        w.drain(64)
    for copy in copies:
        copy.wait_recv()
    return rb0[0, 7, 0] + xb0[1] + xb0[2] + xb0[3], part1[0, 15] + rb1[0, 7] + rb1[1, 6]


QUARTERS = ((0, 0), (0, 1), (1, 1), (1, 0))


def sum_gram(me, w, product, gs, gfull, zbuf, xbuf):
    gram = dot(product, product, ((0,), (0,)))
    for n, (r, h) in enumerate(QUARTERS):
        gs[n] = gram[r * HALF : (r + 1) * HALF, h * HALF : (h + 1) * HALF].reshape(HALF // 8, 8, HALF)

    def tile(ref, z):
        return ref.at[lax.div(z, 4), me.y * 4 + lax.rem(z, 4)]

    far = [8] + [d for r in range(7, 0, -1) for d in (r, ZS - r)]
    copies = [w.go(tile(gs, me.zat(d)), zbuf.at[d], me.zdev(d)) for d in far]
    yield
    total = gs[lax.div(me.z, 4), me.y * 4 + lax.rem(me.z, 4)]
    for d, copy in reversed(list(zip(far, copies))):
        copy.wait_recv()
        total = total + zbuf[d]
    xbuf[me.x] = total
    copies = [w.go(xbuf.at[me.x], xbuf.at[me.x], me.xdev(d)) for d in (2, 1, 3)]
    yield
    for copy in copies:
        copy.wait_recv()
    gfull[lax.div(me.z, 4), me.y * 4 + lax.rem(me.z, 4)] = xbuf[0] + xbuf[1] + xbuf[2] + xbuf[3]
    copies = [w.go(tile(gfull, me.z), tile(gfull, me.z), me.zdev(d)) for d in far]
    yield
    for copy in reversed(copies):
        copy.wait_recv()
    mine = gfull.at[pl.ds(0, 3), pl.ds(me.y * 4, 4)]
    copies = [w.go(mine, mine, me.ydev(d)) for d in (2, 1, 3)]
    yield
    for copy in copies:
        copy.wait_recv()


def kernel(grad, mom, basis, new_mom, new_basis, update,
           gbuf, mbuf, bfull0, bslots1, bfull1, part, rs, q, p1, p2, a, w1, w2, wide,
           gs, gfull, zbuf, xbuf, gs2, gfull2, zbuf2, xbuf2,
           part0, part1, tmp, full0, slots1, full1, rb0, xb0, rb1, half1, whole1, cols0, cols1, sq, out,
           send, recv, local):
    me = Place()
    w = Wires(send, recv)
    loads = [pltpu.make_async_copy(grad, gbuf, local.at[0]), pltpu.make_async_copy(mom, mbuf, local.at[1])]
    for load in loads:
        load.start()
    greet([me.zdev(d) for d in range(1, ZS)] + [me.xdev(d) for d in range(1, XS)] + [me.tdev(d) for d in range(1, TP)])

    share = part.shape[2]

    def multiply(l):
        total = jnp.zeros((part.shape[1] * share, RANK), F32)
        for e in range(XS):
            total = total + dot(gbuf[l, :, me.cols(e)], gathered(bfull0, bfull1, l, e), ((1,), (0,)))
        part[l] = total.reshape(part.shape[1], share, RANK)

    def beside_basis(s):
        if s == 0:
            for load in loads:
                load.wait()
            gbuf[...] = gbuf[...] + mbuf[...]
        if s == 9:
            multiply(0)

    gather_plane(me, w, basis[0], basis[1], bfull0, bslots1, bfull1, beside_basis)
    multiply(1)
    copies = []
    away = (4, 3, 5, 2, 6, 1, 7)
    for d in away:
        there = lax.rem(me.t + d, TP)
        copies.append(w.go(part.at[lax.rem(there, CS), lax.div(there, CS)], rs.at[d], me.tdev(d)))
    total = part[me.c, me.y]
    for d, copy in zip(away, copies):
        copy.wait_recv()
        total = total + rs[d]
    q[me.c, me.y] = total
    copies = [w.go(q.at[me.c, me.y], q.at[me.c, me.y], me.ydev(d)) for d in (2, 1, 3)]
    for copy in copies:
        copy.wait_recv()
    swap = w.go(q.at[me.c], q.at[me.c], me.cdev())

    def take(gram):
        for n, (r, h) in enumerate(QUARTERS):
            quarter = gram[n].reshape(HALF, HALF) if n < 3 else jnp.zeros((HALF, HALF), F32)
            a[r * HALF : (r + 1) * HALF, h * HALF : (h + 1) * HALF] = quarter

    sums = [sum_gram(me, w, q[me.c].reshape(YS * share, RANK), gs, gfull, zbuf, xbuf)]
    next(sums[0])
    swap.wait_recv()
    trade = []

    def fill0():
        for e in range(XS):
            cols = dot(gbuf[0, :, me.cols(e)], q[0].reshape(YS * share, RANK), ((0,), (0,)))
            part0[:, e] = cols.reshape(ZS, 16, RANK)

    def fill1(e):
        cols = dot(gbuf[1, :, me.cols(e)], q[1].reshape(YS * share, RANK), ((0,), (0,)))
        tmp[...] = cols.reshape(ZS, 16, RANK)
        for slot, d in enumerate(FAR):
            part1[e, slot] = tmp[me.zat(d)]

    def beside_scatter(s):
        if s in (1, 2, 4, 6):
            next(sums[0], None)
        if s == 6:
            take(gfull)
        for n in {7: (0, 1, 2), 8: (3, 4, 5), 9: (6, 7)}.get(s, ()):
            eliminate(a, w1, n * PANEL)
        if s == 9:
            p1[...] = dot(q[me.c].reshape(YS * share, RANK), w1[...], ((1,), (1,)))
            sums.append(sum_gram(me, w, p1[...], gs2, gfull2, zbuf2, xbuf2))
            next(sums[1])

    def beside_gather(s):
        if s in (0, 1, 3, 5):
            next(sums[1], None)
        if s == 5:
            take(gfull2)
        for n in {5: (0, 1), 6: (2, 3), 9: (4, 5, 6, 7)}.get(s, ()):
            eliminate(a, w2, n * PANEL)
        if s == 9:
            wide[me.c] = dot(w2[...], w1[...], ((1,), (0,)))
            trade.append(w.go(wide.at[me.c], wide.at[me.c], me.cdev()))
            p2[me.c] = dot(p1[...], w2[...], ((1,), (1,)))
            trade.append(w.go(p2.at[me.c], p2.at[me.c], me.cdev()))

    def finish(l):
        squares = jnp.zeros((1, RANK), F32)
        for e in range(XS):
            block = dot(gathered(full0, full1, l, e), wide[l], ((1,), (1,)))
            if l == 0:
                cols0[:, e] = block.reshape(ZS, 16, RANK)
            else:
                cols1[e] = block.reshape(ZS, 16, RANK)
            squares = squares + jnp.sum(block * block, 0, keepdims=True)
        sq[me.t, l] = jnp.broadcast_to(squares, (8, RANK))

    own = scatter_plane(me, w, part0, part1, rb0, xb0, rb1, half1, whole1, fill0, fill1, beside_scatter)
    gather_plane(me, w, own[0], own[1], full0, slots1, full1, beside_gather)
    for copy in trade:
        copy.wait_recv()
    finish(0)
    finish(1)
    stores = []
    copies = [w.go(sq.at[me.t], sq.at[me.t], me.tdev(d)) for d in range(1, TP)]
    for l in range(LAYERS):
        for e in range(XS):
            block = gathered(cols0, cols1, l, e)
            mbuf[l, :, me.cols(e)] = gbuf[l, :, me.cols(e)] - (1.0 - keep_rate) * dot3(p2[l], block, 1)
        stores.append(pltpu.make_async_copy(mbuf.at[l], new_mom.at[l], local.at[2 + l]))
        stores[-1].start()
    for copy in copies:
        copy.wait_recv()
    for l in range(LAYERS):
        squares = sq[0, l]
        for t in range(1, TP):
            squares = squares + sq[t, l]
        norm = jnp.sqrt(squares[0:1] + eps)
        new_basis[l] = (cols0[me.z, 0] if l == 0 else cols1[0, me.z]) / norm
        scaled = p2[l] * (math.sqrt(ROWS * COLS / RANK) / norm)
        for e in range(XS):
            out[l, :, me.cols(e)] = dot3(scaled, gathered(cols0, cols1, l, e), 1)
        stores.append(pltpu.make_async_copy(out.at[l], update.at[l], local.at[4 + l]))
        stores[-1].start()
    w.drain()
    for store in stores:
        store.wait()


PANEL = 32


def split3(a):
    high = a.astype(BF16)
    rest = a - high.astype(F32)
    mid = rest.astype(BF16)
    low = (rest - mid.astype(F32)).astype(BF16)
    return high, mid, low


def eliminate(a_ref, w_ref, r0):
    halves = [a_ref[r0 : r0 + PANEL, h * HALF : (h + 1) * HALF] for h in (0, 1)]
    finished = []
    for j0 in range(r0, r0 + PANEL, 8):
        side, start = divmod(j0, HALF)
        height = r0 + PANEL - j0
        lane = lax.broadcasted_iota(jnp.int32, (height, HALF), 1)
        row = lax.broadcasted_iota(jnp.int32, (height, HALF), 0)
        cols = [jnp.broadcast_to(halves[side][:, start + k : start + k + 1], (height, HALF)) for k in range(8)]
        scale = jnp.zeros((8, HALF), F32)
        for k in range(8):
            pivot = cols[k][k : k + 1]
            ratio = jnp.where(row > k, cols[k] * (1.0 / pivot), 0.0)
            scale = jnp.where(row[:8] == k, lax.rsqrt(pivot), scale)
            for n in range(k + 1, 8):
                cols[n] = cols[n] - ratio * cols[n][k : k + 1]
            for h in (0, 1):
                kept, spread = halves[h], halves[h][k : k + 1]
                if h == side:
                    spread = jnp.where(lane[0:1] == start + k, 1.0, spread)
                    kept = jnp.where((lane == start + k) & (row >= k), jnp.where(row == k, 1.0, 0.0), kept)
                halves[h] = kept - ratio * spread
        finished.append([half[:8] * scale for half in halves])
        halves = [half[8:] for half in halves] if height > 8 else None
    whole = jnp.concatenate([jnp.concatenate(rows, 1) for rows in finished], 0)
    lanes = lax.broadcasted_iota(jnp.int32, (PANEL, RANK), 1)
    rows = lax.broadcasted_iota(jnp.int32, (PANEL, RANK), 0) + r0
    w_ref[r0 : r0 + PANEL, :] = jnp.where(lanes <= rows, whole, 0.0)
    rest = r0 + PANEL
    if rest < RANK:
        right = jnp.where((lanes > rows) & (lanes < rest), 0.0, whole)
        h, m, l = split3(whole)
        hr, mr, lr = split3(right)
        left = jnp.concatenate([h, h, m, h, l, m], 0)
        base = rest // HALF * HALF
        change = lax.dot_general(
            left[:, base:], jnp.concatenate([hr, mr, hr, lr, hr, mr], 0),
            (((0,), (0,)), ((), ())), preferred_element_type=F32)
        wide = lax.broadcasted_iota(jnp.int32, (RANK - rest, RANK), 1)
        old = jnp.where((wide >= r0) & (wide < rest), 0.0, a_ref[rest:, :])
        a_ref[rest:, :] = old - change[rest - base :, :]


def hand_over(a, b, c, a_out, b_out, c_out):
    a_out[...] = a[...]
    b_out[...] = b[...]
    c_out[...] = c[...]


def vmem(*shape):
    return pltpu.VMEM(shape, F32)


V = pl.BlockSpec(memory_space=pltpu.VMEM)
ANY = pl.BlockSpec(memory_space=pl.ANY)
COPIES = 288


def per_device(gradient, momentum, basis):
    rows, cols = gradient.shape[1:]
    share = basis.shape[1]
    whole = jax.ShapeDtypeStruct((LAYERS, rows, cols), F32)
    plane = [vmem(ZS, XS, share, RANK), vmem(XS, ZS, share, RANK), vmem(XS, ZS, share, RANK)]
    sums = [vmem(4, HALF // 8, 8, HALF), vmem(4, HALF // 8, 8, HALF), vmem(ZS, 8, HALF), vmem(XS, 8, HALF)]
    shapes = (whole, jax.ShapeDtypeStruct((LAYERS, share, RANK), F32), whole)
    results = pl.pallas_call(
        kernel,
        out_shape=shapes,
        in_specs=[ANY, ANY, V],
        out_specs=(ANY, V, ANY),
        scratch_shapes=[
            vmem(LAYERS, rows, cols), vmem(LAYERS, rows, cols), *plane,
            vmem(LAYERS, YS, rows // YS, RANK), vmem(TP, rows // YS, RANK), vmem(LAYERS, YS, rows // YS, RANK),
            vmem(rows, RANK), vmem(LAYERS, rows, RANK),
            vmem(RANK, RANK), vmem(RANK, RANK), vmem(RANK, RANK), vmem(LAYERS, RANK, RANK),
            *sums, *sums,
            vmem(ZS, XS, share, RANK), vmem(XS, ZS, share, RANK), vmem(ZS, share, RANK), *plane,
            vmem(2, 8, XS, share, RANK), vmem(XS, share, RANK), vmem(2, 8, share, RANK),
            vmem(ZS, share, RANK), vmem(2, ZS, share, RANK),
            vmem(ZS, XS, share, RANK), vmem(XS, ZS, share, RANK), vmem(TP, LAYERS, 8, RANK), vmem(LAYERS, rows, cols),
            pltpu.SemaphoreType.DMA((COPIES,)), pltpu.SemaphoreType.DMA((COPIES,)), pltpu.SemaphoreType.DMA((6,)),
        ],
        compiler_params=pltpu.CompilerParams(
            collective_id=0, has_side_effects=True, vmem_limit_bytes=60 * 2**20),
        name="step",
    )(gradient, momentum, basis)
    return pl.pallas_call(
        hand_over,
        out_shape=shapes,
        grid=(LAYERS,),
        in_specs=[pl.BlockSpec((1,) + shape.shape[1:], lambda l: (l, 0, 0)) for shape in shapes],
        out_specs=tuple(pl.BlockSpec((1,) + shape.shape[1:], lambda l: (l, 0, 0)) for shape in shapes),
        compiler_params=pltpu.CompilerParams(vmem_limit_bytes=60 * 2**20),
        name="hand_over",
    )(*results)


def solution(mesh):
    return jax.shard_map(
        per_device,
        mesh=mesh,
        in_specs=(P(None, "fsdp", "tp"), P(None, "fsdp", "tp"), P(None, ("tp", "fsdp"), None)),
        out_specs=(P(None, "fsdp", "tp"), P(None, ("tp", "fsdp"), None), P(None, "fsdp", "tp")),
        check_vma=False,
    )
```

```python
import math

import jax
import jax.numpy as jnp
from jax import lax
from jax.experimental import pallas as pl
from jax.experimental.pallas import tpu as pltpu
from jax.sharding import PartitionSpec as P

ROWS = 8192
COLS = 8192
RANK = 256
LAYERS = 2
XS, ZS, YS, CS = 4, 16, 4, 2
TP = YS * CS
MESH = pl.DeviceIdType.MESH
HIGHEST = lax.Precision.HIGHEST
F32 = jnp.float32
BF16 = jnp.bfloat16
HALF = RANK // 2

keep_rate = 0.95
eps = 1e-06


def dot(a, b, dims):
    return lax.dot_general(a, b, (dims, ((), ())), precision=HIGHEST, preferred_element_type=F32)


def split2(a):
    high = a.astype(BF16)
    return high, (a - high.astype(F32)).astype(BF16)


def dot3(a, b, axis):
    ah, al = split2(a)
    bh, bl = split2(b)
    return lax.dot_general(
        jnp.concatenate([ah, ah, al], axis), jnp.concatenate([bh, bl, bh], axis),
        (((axis,), (axis,)), ((), ())), preferred_element_type=F32)


class Place:
    def __init__(self):
        self.f = lax.axis_index("fsdp")
        self.t = lax.axis_index("tp")
        self.x = lax.div(self.f, ZS)
        self.z = lax.rem(self.f, ZS)
        self.y = lax.div(self.t, CS)
        self.c = lax.rem(self.t, CS)

    def zat(self, d):
        return lax.rem(self.z + (ZS + d), ZS)

    def xat(self, d):
        return lax.rem(self.x + (XS + d), XS)

    def yat(self, d):
        return lax.rem(self.y + (YS + d), YS)

    def cols(self, e):
        return pl.ds(pl.multiple_of(self.xat(e) * 256, 256), 256)

    def zdev(self, d):
        return (self.x * ZS + self.zat(d), self.t)

    def xdev(self, d):
        return (self.xat(d) * ZS + self.z, self.t)

    def tdev(self, d):
        return (self.f, lax.rem(self.t + (TP + d), TP))

    def ydev(self, d):
        return (self.f, self.yat(d) * CS + self.c)

    def cdev(self):
        return (self.f, self.y * CS + (1 - self.c))


class Wires:
    def __init__(self, send, recv):
        self.send, self.recv, self.used = send, recv, 0
        self.sent = []

    def go(self, src, dst, device):
        i = self.used
        self.used += 1
        copy = pltpu.make_async_remote_copy(
            src_ref=src, dst_ref=dst, send_sem=self.send.at[i], recv_sem=self.recv.at[i],
            device_id=device, device_id_type=MESH,
        )
        copy.start()
        self.sent.append(copy)
        return copy

    def drain(self, keep=0):
        while len(self.sent) > keep:
            self.sent.pop(0).wait_send()


def gathered(full0, full1, l, e):
    block = full0[:, e] if l == 0 else full1[e]
    return block.reshape(256, RANK)


def greet(devices):
    barrier = pltpu.get_barrier_semaphore()
    for device in devices:
        pl.semaphore_signal(barrier, inc=1, device_id=device, device_id_type=MESH)
    pl.semaphore_wait(barrier, len(devices))


WAYS = ((1, 8), (-1, 7))


def near(way, d):
    return 0 if d == 0 else 2 * d - 1 if way == 1 else 2 * d


STREAMS = {0: ((1, 2), (-1, 2)), -5: ((1, 3), (-1, 2)), 5: ((1, 2), (-1, 2))}


def slot_of(c, way, d):
    return 15 if d == 3 else {0: 0, -5: 5, 5: 10}[c] + near(way, d)


OFFSETS = {slot_of(c, way, d): c - way * d for c in STREAMS for way, hops in STREAMS[c] for d in range(hops + 1)}
GROUPS = ((0, 5), (5, 10), (10, 16))


def gather_plane(me, w, own0, own1, full0, slots1, full1, beside):
    full0[me.z, 0] = own0
    slots1[0, 0] = own1
    full1[0, me.z] = own1
    xa = {e: w.go(full0.at[me.z, 0], full0.at[me.z, (-e) % XS], me.xdev(e)) for e in (3, 1, 2)}
    ring, wide, ahead = {}, {}, {}
    for c in (-5, 5):
        ring["b", c] = w.go(slots1.at[0, 0], slots1.at[0, slot_of(c, 1, 0)], me.zdev(-c))

    def hop_b(s):
        for c, ways in STREAMS.items():
            i = s if c == 0 else s - 2
            if i == 0 and c != 0:
                ring["b", c].wait_recv()
            for way, last in ways:
                if 0 < i <= last:
                    ring["b", c, way, i - 1].wait_recv()
                if 0 <= i < last:
                    ring["b", c, way, i] = w.go(
                        slots1.at[0, slot_of(c, way, i)], slots1.at[0, slot_of(c, way, i + 1)], me.zdev(way))

    def hop_a(s):
        for half in (0, 1):
            pair = pl.ds(2 * half, 2)
            if s == 0:
                for e in ((3,), (1, 2))[half]:
                    xa[e].wait_recv()
                block = full0.at[me.z, pair]
                for c in (-5, 5):
                    ring["a", c, half] = w.go(block, block, me.zdev(-c))
            for c, ways in STREAMS.items():
                i = s if c == 0 else s - 3
                if i == 0 and c != 0:
                    ring["a", c, half].wait_recv()
                for way, last in ways:
                    if 0 < i <= last:
                        ring["a", c, way, i - 1, half].wait_recv()
                    if 0 <= i < last:
                        block = full0.at[me.zat(c - way * i), pair]
                        ring["a", c, way, i, half] = w.go(block, block, me.zdev(way))

    def spread(g):
        lo, hi = GROUPS[g]
        group = slots1.at[0, pl.ds(lo, hi - lo)]
        wide[g] = [w.go(group, slots1.at[(-e) % XS, pl.ds(lo, hi - lo)], me.xdev(e)) for e in (1, -1)]
        for i in range(lo, hi):
            full1[0, me.zat(OFFSETS[i])] = slots1[0, i]

    def forward(g):
        lo, hi = GROUPS[g]
        mid = (lo + hi) // 2
        ahead[g] = []
        for n, (a, b, e) in enumerate(((lo, mid, 1), (mid, hi, -1))):
            wide[g][n].wait_recv()
            ahead[g].append(
                w.go(slots1.at[(-e) % XS, pl.ds(a, b - a)], slots1.at[2, pl.ds(a, b - a)], me.xdev(e)))
        for i in range(lo, hi):
            for e in (1, 3):
                full1[e, me.zat(OFFSETS[i])] = slots1[e, i]

    for s in range(7):
        hop_b(s)
        if s in (2, 4, 5):
            spread((2, 4, 5).index(s))
        hop_a(s)
        if s in (4, 6):
            forward(s // 2 - 2)
        beside(s)
        w.drain(64)
    forward(2)
    beside(9)
    for g in range(3):
        for copy in ahead[g]:
            copy.wait_recv()
        for i in range(*GROUPS[g]):
            full1[2, me.zat(OFFSETS[i])] = slots1[2, i]


FAR = [8] + [d for r in range(7, 0, -1) for d in (r, -r)] + [0]
FAR_GROUPS = ((0, 3), (3, 7), (7, 11), (11, 16))


def scatter_plane(me, w, part0, part1, rb0, xb0, rb1, half1, whole1, fill0, fill1, beside):
    first, second, ring = {}, {}, {}

    def begin(g):
        lo, hi = FAR_GROUPS[g]
        mid = (lo + hi) // 2
        first[g] = [
            w.go(part1.at[2, pl.ds(a, b - a)], half1.at[pl.ds(a, b - a)], me.xdev(e))
            for a, b, e in ((lo, mid, 1), (mid, hi, -1))
        ]

    def pass_on(g):
        lo, hi = FAR_GROUPS[g]
        mid = (lo + hi) // 2
        second[g] = []
        for n, (a, b, e) in enumerate(((lo, mid, 1), (mid, hi, -1))):
            first[g][n].wait_recv()
            part1[e % XS, a:b] = part1[e % XS, a:b] + half1[a:b]
            second[g].append(
                w.go(part1.at[e % XS, pl.ds(lo, hi - lo)], whole1.at[n, pl.ds(lo, hi - lo)], me.xdev(e)))

    def collect(g):
        lo, hi = FAR_GROUPS[g]
        for copy in second[g]:
            copy.wait_recv()
        part1[0, lo:hi] = part1[0, lo:hi] + whole1[0, lo:hi] + whole1[1, lo:hi]

    def hop_a(s):
        for half in (0, 1):
            lo, hi = 2 * half, 2 * half + 2
            pair = pl.ds(lo, 2)
            for k, (way, last) in enumerate(WAYS):
                if s > last:
                    continue
                there = me.zat(way * (last - s))
                if s == 0:
                    ring["a", way, 0, half] = w.go(part0.at[there, pair], rb0.at[k, 0, pair], me.zdev(way))
                    continue
                ring["a", way, s - 1, half].wait_recv()
                if s < last:
                    rb0[k, s - 1, lo:hi] = rb0[k, s - 1, lo:hi] + part0[there, lo:hi]
                    ring["a", way, s, half] = w.go(rb0.at[k, s - 1, pair], rb0.at[k, s, pair], me.zdev(way))

    def hop_b(s):
        for k, (way, last) in enumerate(WAYS):
            if s > last:
                continue
            slot = FAR.index(way * (last - s))
            if s == 0:
                ring["b", way, 0] = w.go(part1.at[0, slot], rb1.at[k, 0], me.zdev(way))
                continue
            ring["b", way, s - 1].wait_recv()
            if s < last:
                rb1[k, s - 1] = rb1[k, s - 1] + part1[0, slot]
                ring["b", way, s] = w.go(rb1.at[k, s - 1], rb1.at[k, s], me.zdev(way))

    fill1(2)
    for g in range(4):
        begin(g)
    fill0()
    copies = []
    for s in range(11):
        if s <= 8:
            hop_a(s)
        if s == 0:
            fill1(1)
            fill1(3)
        if s == 1:
            fill1(0)
        if s == 8:
            rb0[0, 7] = rb0[0, 7] + part0[me.z] + rb0[1, 6]
            copies = [w.go(rb0.at[0, 7, e], xb0.at[e], me.xdev(e)) for e in (2, 1, 3)]
        if s in (0, 2, 4, 6):
            pass_on(s // 2)
        if s in (1, 3, 5, 7):
            collect(s // 2)
        if s >= 2:
            hop_b(s - 2)
        beside(s)
        w.drain(64)
    for copy in copies:
        copy.wait_recv()
    return rb0[0, 7, 0] + xb0[1] + xb0[2] + xb0[3], part1[0, 15] + rb1[0, 7] + rb1[1, 6]


QUARTERS = ((0, 0), (0, 1), (1, 1), (1, 0))


def sum_gram(me, w, product, gs, gfull, zbuf, xbuf):
    gram = dot(product, product, ((0,), (0,)))
    for n, (r, h) in enumerate(QUARTERS):
        gs[n] = gram[r * HALF : (r + 1) * HALF, h * HALF : (h + 1) * HALF].reshape(HALF // 8, 8, HALF)

    def tile(ref, z):
        return ref.at[lax.div(z, 4), me.y * 4 + lax.rem(z, 4)]

    far = [8] + [d for r in range(7, 0, -1) for d in (r, ZS - r)]
    copies = [w.go(tile(gs, me.zat(d)), zbuf.at[d], me.zdev(d)) for d in far]
    yield
    total = gs[lax.div(me.z, 4), me.y * 4 + lax.rem(me.z, 4)]
    for d, copy in reversed(list(zip(far, copies))):
        copy.wait_recv()
        total = total + zbuf[d]
    xbuf[me.x] = total
    copies = [w.go(xbuf.at[me.x], xbuf.at[me.x], me.xdev(d)) for d in (2, 1, 3)]
    yield
    for copy in copies:
        copy.wait_recv()
    gfull[lax.div(me.z, 4), me.y * 4 + lax.rem(me.z, 4)] = xbuf[0] + xbuf[1] + xbuf[2] + xbuf[3]
    copies = [w.go(tile(gfull, me.z), tile(gfull, me.z), me.zdev(d)) for d in far]
    yield
    for copy in reversed(copies):
        copy.wait_recv()
    mine = gfull.at[pl.ds(0, 3), pl.ds(me.y * 4, 4)]
    copies = [w.go(mine, mine, me.ydev(d)) for d in (2, 1, 3)]
    yield
    for copy in copies:
        copy.wait_recv()


def kernel(grad, mom, basis, new_mom, new_basis, update,
           gbuf, mbuf, bfull0, bslots1, bfull1, part, rs, q, p1, p2, a, w1, w2, turned,
           gs, gfull, zbuf, xbuf, gs2, gfull2, zbuf2, xbuf2,
           part0, part1, tmp, full0, slots1, full1, rb0, xb0, rb1, half1, whole1, cols0, cols1, sq, out,
           send, recv, local):
    me = Place()
    w = Wires(send, recv)
    loads = [pltpu.make_async_copy(grad, gbuf, local.at[0]), pltpu.make_async_copy(mom, mbuf, local.at[1])]
    for load in loads:
        load.start()
    greet([me.zdev(d) for d in range(1, ZS)] + [me.xdev(d) for d in range(1, XS)] + [me.tdev(d) for d in range(1, TP)])

    share = part.shape[2]

    def multiply(l):
        total = jnp.zeros((part.shape[1] * share, RANK), F32)
        for e in range(XS):
            total = total + dot(gbuf[l, :, me.cols(e)], gathered(bfull0, bfull1, l, e), ((1,), (0,)))
        part[l] = total.reshape(part.shape[1], share, RANK)

    def beside_basis(s):
        if s == 0:
            for load in loads:
                load.wait()
            gbuf[...] = gbuf[...] + mbuf[...]
        if s in (1, 2):
            turned[s - 1] = gbuf[s - 1].T
        if s == 9:
            multiply(0)

    gather_plane(me, w, basis[0], basis[1], bfull0, bslots1, bfull1, beside_basis)
    multiply(1)
    copies = []
    away = (4, 3, 5, 2, 6, 1, 7)
    for d in away:
        there = lax.rem(me.t + d, TP)
        copies.append(w.go(part.at[lax.rem(there, CS), lax.div(there, CS)], rs.at[d], me.tdev(d)))
    total = part[me.c, me.y]
    for d, copy in zip(away, copies):
        copy.wait_recv()
        total = total + rs[d]
    q[me.c, me.y] = total
    copies = [w.go(q.at[me.c, me.y], q.at[me.c, me.y], me.ydev(d)) for d in (2, 1, 3)]
    for copy in copies:
        copy.wait_recv()
    swap = w.go(q.at[me.c], q.at[me.c], me.cdev())

    def take(gram):
        for n, (r, h) in enumerate(QUARTERS):
            quarter = gram[n].reshape(HALF, HALF) if n < 3 else jnp.zeros((HALF, HALF), F32)
            a[r * HALF : (r + 1) * HALF, h * HALF : (h + 1) * HALF] = quarter

    sums = [sum_gram(me, w, q[me.c].reshape(YS * share, RANK), gs, gfull, zbuf, xbuf)]
    next(sums[0])
    swap.wait_recv()
    trade = []

    def fill0():
        for e in range(XS):
            cols = dot(turned[0, me.cols(e)], q[0].reshape(YS * share, RANK), ((1,), (0,)))
            part0[:, e] = cols.reshape(ZS, 16, RANK)

    def fill1(e):
        cols = dot(turned[1, me.cols(e)], q[1].reshape(YS * share, RANK), ((1,), (0,)))
        tmp[...] = cols.reshape(ZS, 16, RANK)
        for slot, d in enumerate(FAR):
            part1[e, slot] = tmp[me.zat(d)]

    def beside_scatter(s):
        if s in (1, 2, 4, 6):
            next(sums[0], None)
        if s == 6:
            take(gfull)
        for n in {7: (0, 1, 2), 8: (3, 4, 5), 9: (6, 7)}.get(s, ()):
            eliminate(a, w1.at[me.c], n * PANEL)
        if s == 9:
            trade.append(w.go(w1.at[me.c], w1.at[me.c], me.cdev()))
            p1[...] = dot(q[me.c].reshape(YS * share, RANK), w1[me.c], ((1,), (1,)))
            sums.append(sum_gram(me, w, p1[...], gs2, gfull2, zbuf2, xbuf2))
            next(sums[1])

    def beside_gather(s):
        if s in (0, 1, 2, 4):
            next(sums[1], None)
        if s == 4:
            take(gfull2)
        for n in {4: (0, 1), 5: (2, 3), 6: (4, 5), 9: (6, 7)}.get(s, ()):
            eliminate(a, w2.at[me.c], n * PANEL)
        if s == 9:
            trade.append(w.go(w2.at[me.c], w2.at[me.c], me.cdev()))
            p2[me.c] = dot(p1[...], w2[me.c], ((1,), (1,)))
            trade.append(w.go(p2.at[me.c], p2.at[me.c], me.cdev()))

    def finish(l):
        squares = jnp.zeros((1, RANK), F32)
        for e in range(XS):
            block = dot3(gathered(full0, full1, l, e), w2[l], 1)
            if l == 0:
                cols0[:, e] = block.reshape(ZS, 16, RANK)
            else:
                cols1[e] = block.reshape(ZS, 16, RANK)
            squares = squares + jnp.sum(block * block, 0, keepdims=True)
        sq[me.t, l] = jnp.broadcast_to(squares, (8, RANK))

    own = scatter_plane(me, w, part0, part1, rb0, xb0, rb1, half1, whole1, fill0, fill1, beside_scatter)
    trade[0].wait_recv()
    own = [dot(own[l], w1[l], ((1,), (1,))) for l in range(LAYERS)]
    gather_plane(me, w, own[0], own[1], full0, slots1, full1, beside_gather)
    for copy in trade[1:]:
        copy.wait_recv()
    finish(0)
    finish(1)
    stores = []
    copies = [w.go(sq.at[me.t], sq.at[me.t], me.tdev(d)) for d in range(1, TP)]
    for l in range(LAYERS):
        for e in range(XS):
            block = gathered(cols0, cols1, l, e)
            mbuf[l, :, me.cols(e)] = gbuf[l, :, me.cols(e)] - (1.0 - keep_rate) * dot3(p2[l], block, 1)
        stores.append(pltpu.make_async_copy(mbuf.at[l], new_mom.at[l], local.at[2 + l]))
        stores[-1].start()
    for copy in copies:
        copy.wait_recv()
    for l in range(LAYERS):
        squares = sq[0, l]
        for t in range(1, TP):
            squares = squares + sq[t, l]
        norm = jnp.sqrt(squares[0:1] + eps)
        new_basis[l] = (cols0[me.z, 0] if l == 0 else cols1[0, me.z]) / norm
        scaled = p2[l] * (math.sqrt(ROWS * COLS / RANK) / norm)
        for e in range(XS):
            out[l, :, me.cols(e)] = dot3(scaled, gathered(cols0, cols1, l, e), 1)
        stores.append(pltpu.make_async_copy(out.at[l], update.at[l], local.at[4 + l]))
        stores[-1].start()
    w.drain()
    for store in stores:
        store.wait()


PANEL = 32


def split3(a):
    high = a.astype(BF16)
    rest = a - high.astype(F32)
    mid = rest.astype(BF16)
    low = (rest - mid.astype(F32)).astype(BF16)
    return high, mid, low


def eliminate(a_ref, w_ref, r0):
    halves = [a_ref[r0 : r0 + PANEL, h * HALF : (h + 1) * HALF] for h in (0, 1)]
    finished = []
    for j0 in range(r0, r0 + PANEL, 8):
        side, start = divmod(j0, HALF)
        height = r0 + PANEL - j0
        lane = lax.broadcasted_iota(jnp.int32, (height, HALF), 1)
        row = lax.broadcasted_iota(jnp.int32, (height, HALF), 0)
        cols = [jnp.broadcast_to(halves[side][:, start + k : start + k + 1], (height, HALF)) for k in range(8)]
        scale = jnp.zeros((8, HALF), F32)
        for k in range(8):
            pivot = cols[k][k : k + 1]
            ratio = jnp.where(row > k, cols[k] * (1.0 / pivot), 0.0)
            scale = jnp.where(row[:8] == k, lax.rsqrt(pivot), scale)
            for n in range(k + 1, 8):
                cols[n] = cols[n] - ratio * cols[n][k : k + 1]
            for h in (0, 1):
                kept, spread = halves[h], halves[h][k : k + 1]
                if h == side:
                    spread = jnp.where(lane[0:1] == start + k, 1.0, spread)
                    kept = jnp.where((lane == start + k) & (row >= k), jnp.where(row == k, 1.0, 0.0), kept)
                halves[h] = kept - ratio * spread
        finished.append([half[:8] * scale for half in halves])
        halves = [half[8:] for half in halves] if height > 8 else None
    whole = jnp.concatenate([jnp.concatenate(rows, 1) for rows in finished], 0)
    lanes = lax.broadcasted_iota(jnp.int32, (PANEL, RANK), 1)
    rows = lax.broadcasted_iota(jnp.int32, (PANEL, RANK), 0) + r0
    w_ref[r0 : r0 + PANEL, :] = jnp.where(lanes <= rows, whole, 0.0)
    rest = r0 + PANEL
    if rest < RANK:
        right = jnp.where((lanes > rows) & (lanes < rest), 0.0, whole)
        h, m, l = split3(whole)
        hr, mr, lr = split3(right)
        left = jnp.concatenate([h, h, m, h, l, m], 0)
        base = rest // HALF * HALF
        change = lax.dot_general(
            left[:, base:], jnp.concatenate([hr, mr, hr, lr, hr, mr], 0),
            (((0,), (0,)), ((), ())), preferred_element_type=F32)
        wide = lax.broadcasted_iota(jnp.int32, (RANK - rest, RANK), 1)
        old = jnp.where((wide >= r0) & (wide < rest), 0.0, a_ref[rest:, :])
        a_ref[rest:, :] = old - change[rest - base :, :]


def hand_over(a, b, c, a_out, b_out, c_out):
    a_out[...] = a[...]
    b_out[...] = b[...]
    c_out[...] = c[...]


def vmem(*shape):
    return pltpu.VMEM(shape, F32)


V = pl.BlockSpec(memory_space=pltpu.VMEM)
ANY = pl.BlockSpec(memory_space=pl.ANY)
COPIES = 288


def per_device(gradient, momentum, basis):
    rows, cols = gradient.shape[1:]
    share = basis.shape[1]
    whole = jax.ShapeDtypeStruct((LAYERS, rows, cols), F32)
    plane = [vmem(ZS, XS, share, RANK), vmem(XS, ZS, share, RANK), vmem(XS, ZS, share, RANK)]
    sums = [vmem(4, HALF // 8, 8, HALF), vmem(4, HALF // 8, 8, HALF), vmem(ZS, 8, HALF), vmem(XS, 8, HALF)]
    shapes = (whole, jax.ShapeDtypeStruct((LAYERS, share, RANK), F32), whole)
    results = pl.pallas_call(
        kernel,
        out_shape=shapes,
        in_specs=[ANY, ANY, V],
        out_specs=(ANY, V, ANY),
        scratch_shapes=[
            vmem(LAYERS, rows, cols), vmem(LAYERS, rows, cols), *plane,
            vmem(LAYERS, YS, rows // YS, RANK), vmem(TP, rows // YS, RANK), vmem(LAYERS, YS, rows // YS, RANK),
            vmem(rows, RANK), vmem(LAYERS, rows, RANK),
            vmem(RANK, RANK), vmem(LAYERS, RANK, RANK), vmem(LAYERS, RANK, RANK), vmem(LAYERS, cols, rows),
            *sums, *sums,
            vmem(ZS, XS, share, RANK), vmem(XS, ZS, share, RANK), vmem(ZS, share, RANK), *plane,
            vmem(2, 8, XS, share, RANK), vmem(XS, share, RANK), vmem(2, 8, share, RANK),
            vmem(ZS, share, RANK), vmem(2, ZS, share, RANK),
            vmem(ZS, XS, share, RANK), vmem(XS, ZS, share, RANK), vmem(TP, LAYERS, 8, RANK), vmem(LAYERS, rows, cols),
            pltpu.SemaphoreType.DMA((COPIES,)), pltpu.SemaphoreType.DMA((COPIES,)), pltpu.SemaphoreType.DMA((6,)),
        ],
        compiler_params=pltpu.CompilerParams(
            collective_id=0, has_side_effects=True, vmem_limit_bytes=60 * 2**20),
        name="step",
    )(gradient, momentum, basis)
    return pl.pallas_call(
        hand_over,
        out_shape=shapes,
        grid=(LAYERS,),
        in_specs=[pl.BlockSpec((1,) + shape.shape[1:], lambda l: (l, 0, 0)) for shape in shapes],
        out_specs=tuple(pl.BlockSpec((1,) + shape.shape[1:], lambda l: (l, 0, 0)) for shape in shapes),
        compiler_params=pltpu.CompilerParams(vmem_limit_bytes=60 * 2**20),
        name="hand_over",
    )(*results)


def solution(mesh):
    return jax.shard_map(
        per_device,
        mesh=mesh,
        in_specs=(P(None, "fsdp", "tp"), P(None, "fsdp", "tp"), P(None, ("tp", "fsdp"), None)),
        out_specs=(P(None, "fsdp", "tp"), P(None, ("tp", "fsdp"), None), P(None, "fsdp", "tp")),
        check_vma=False,
    )
```

```python
import math

import jax
import jax.numpy as jnp
from jax import lax
from jax.experimental import pallas as pl
from jax.experimental.pallas import tpu as pltpu
from jax.sharding import PartitionSpec as P

ROWS = 8192
COLS = 8192
RANK = 256
LAYERS = 2
XS, ZS, YS, CS = 4, 16, 4, 2
TP = YS * CS
MESH = pl.DeviceIdType.MESH
HIGHEST = lax.Precision.HIGHEST
F32 = jnp.float32
BF16 = jnp.bfloat16
HALF = RANK // 2

keep_rate = 0.95
eps = 1e-06


def dot(a, b, dims):
    return lax.dot_general(a, b, (dims, ((), ())), precision=HIGHEST, preferred_element_type=F32)


def split2(a):
    high = a.astype(BF16)
    return high, (a - high.astype(F32)).astype(BF16)


def dot3(a, b, axis):
    ah, al = split2(a)
    bh, bl = split2(b)
    return lax.dot_general(
        jnp.concatenate([ah, ah, al], axis), jnp.concatenate([bh, bl, bh], axis),
        (((axis,), (axis,)), ((), ())), preferred_element_type=F32)


class Place:
    def __init__(self):
        self.f = lax.axis_index("fsdp")
        self.t = lax.axis_index("tp")
        self.x = lax.div(self.f, ZS)
        self.z = lax.rem(self.f, ZS)
        self.y = lax.div(self.t, CS)
        self.c = lax.rem(self.t, CS)

    def zat(self, d):
        return lax.rem(self.z + (ZS + d), ZS)

    def xat(self, d):
        return lax.rem(self.x + (XS + d), XS)

    def yat(self, d):
        return lax.rem(self.y + (YS + d), YS)

    def cols(self, e):
        return pl.ds(pl.multiple_of(self.xat(e) * 256, 256), 256)

    def zdev(self, d):
        return (self.x * ZS + self.zat(d), self.t)

    def xdev(self, d):
        return (self.xat(d) * ZS + self.z, self.t)

    def tdev(self, d):
        return (self.f, lax.rem(self.t + (TP + d), TP))

    def ydev(self, d):
        return (self.f, self.yat(d) * CS + self.c)

    def cdev(self):
        return (self.f, self.y * CS + (1 - self.c))


class Wires:
    def __init__(self, send, recv):
        self.send, self.recv, self.used = send, recv, 0
        self.sent = []

    def go(self, src, dst, device):
        i = self.used
        self.used += 1
        copy = pltpu.make_async_remote_copy(
            src_ref=src, dst_ref=dst, send_sem=self.send.at[i], recv_sem=self.recv.at[i],
            device_id=device, device_id_type=MESH,
        )
        copy.start()
        self.sent.append(copy)
        return copy

    def drain(self, keep=0):
        while len(self.sent) > keep:
            self.sent.pop(0).wait_send()


def gathered(full0, full1, l, e):
    block = full0[:, e] if l == 0 else full1[e]
    return block.reshape(256, RANK)


def greet(devices):
    barrier = pltpu.get_barrier_semaphore()
    for device in devices:
        pl.semaphore_signal(barrier, inc=1, device_id=device, device_id_type=MESH)
    pl.semaphore_wait(barrier, len(devices))


WAYS = ((1, 8), (-1, 7))


def near(way, d):
    return 0 if d == 0 else 2 * d - 1 if way == 1 else 2 * d


STREAMS = {0: ((1, 2), (-1, 2)), -5: ((1, 3), (-1, 2)), 5: ((1, 2), (-1, 2))}


def slot_of(c, way, d):
    return 15 if d == 3 else {0: 0, -5: 5, 5: 10}[c] + near(way, d)


OFFSETS = {slot_of(c, way, d): c - way * d for c in STREAMS for way, hops in STREAMS[c] for d in range(hops + 1)}
GROUPS = ((0, 5), (5, 10), (10, 16))


def gather_plane(me, w, own0, own1, full0, slots1, full1, beside):
    full0[me.z, 0] = own0
    slots1[0, 0] = own1
    full1[0, me.z] = own1
    xa = {e: w.go(full0.at[me.z, 0], full0.at[me.z, (-e) % XS], me.xdev(e)) for e in (3, 1, 2)}
    ring, wide, ahead = {}, {}, {}
    for c in (-5, 5):
        ring["b", c] = w.go(slots1.at[0, 0], slots1.at[0, slot_of(c, 1, 0)], me.zdev(-c))

    def hop_b(s):
        for c, ways in STREAMS.items():
            i = s if c == 0 else s - 2
            if i == 0 and c != 0:
                ring["b", c].wait_recv()
            for way, last in ways:
                if 0 < i <= last:
                    ring["b", c, way, i - 1].wait_recv()
                if 0 <= i < last:
                    ring["b", c, way, i] = w.go(
                        slots1.at[0, slot_of(c, way, i)], slots1.at[0, slot_of(c, way, i + 1)], me.zdev(way))

    def hop_a(s):
        for half in (0, 1):
            pair = pl.ds(2 * half, 2)
            if s == 0:
                for e in ((3,), (1, 2))[half]:
                    xa[e].wait_recv()
                block = full0.at[me.z, pair]
                for c in (-5, 5):
                    ring["a", c, half] = w.go(block, block, me.zdev(-c))
            for c, ways in STREAMS.items():
                i = s if c == 0 else s - 3
                if i == 0 and c != 0:
                    ring["a", c, half].wait_recv()
                for way, last in ways:
                    if 0 < i <= last:
                        ring["a", c, way, i - 1, half].wait_recv()
                    if 0 <= i < last:
                        block = full0.at[me.zat(c - way * i), pair]
                        ring["a", c, way, i, half] = w.go(block, block, me.zdev(way))

    def spread(g):
        lo, hi = GROUPS[g]
        group = slots1.at[0, pl.ds(lo, hi - lo)]
        wide[g] = [w.go(group, slots1.at[(-e) % XS, pl.ds(lo, hi - lo)], me.xdev(e)) for e in (1, -1)]
        for i in range(lo, hi):
            full1[0, me.zat(OFFSETS[i])] = slots1[0, i]

    def forward(g):
        lo, hi = GROUPS[g]
        mid = (lo + hi) // 2
        ahead[g] = []
        for n, (a, b, e) in enumerate(((lo, mid, 1), (mid, hi, -1))):
            wide[g][n].wait_recv()
            ahead[g].append(
                w.go(slots1.at[(-e) % XS, pl.ds(a, b - a)], slots1.at[2, pl.ds(a, b - a)], me.xdev(e)))
        for i in range(lo, hi):
            for e in (1, 3):
                full1[e, me.zat(OFFSETS[i])] = slots1[e, i]

    for s in range(7):
        hop_b(s)
        if s in (2, 4, 5):
            spread((2, 4, 5).index(s))
        hop_a(s)
        if s in (4, 6):
            forward(s // 2 - 2)
        beside(s)
        w.drain(64)
    forward(2)
    beside(9)
    for g in range(3):
        for copy in ahead[g]:
            copy.wait_recv()
        for i in range(*GROUPS[g]):
            full1[2, me.zat(OFFSETS[i])] = slots1[2, i]


FAR = [8] + [d for r in range(7, 0, -1) for d in (r, -r)] + [0]
FAR_GROUPS = ((0, 3), (3, 7), (7, 11), (11, 16))


def scatter_plane(me, w, part0, part1, rb0, xb0, rb1, half1, whole1, fill0, fill1, beside):
    first, second, ring = {}, {}, {}

    def begin(g):
        lo, hi = FAR_GROUPS[g]
        mid = (lo + hi) // 2
        first[g] = [
            w.go(part1.at[2, pl.ds(a, b - a)], half1.at[pl.ds(a, b - a)], me.xdev(e))
            for a, b, e in ((lo, mid, 1), (mid, hi, -1))
        ]

    def pass_on(g):
        lo, hi = FAR_GROUPS[g]
        mid = (lo + hi) // 2
        second[g] = []
        for n, (a, b, e) in enumerate(((lo, mid, 1), (mid, hi, -1))):
            first[g][n].wait_recv()
            part1[e % XS, a:b] = part1[e % XS, a:b] + half1[a:b]
            second[g].append(
                w.go(part1.at[e % XS, pl.ds(lo, hi - lo)], whole1.at[n, pl.ds(lo, hi - lo)], me.xdev(e)))

    def collect(g):
        lo, hi = FAR_GROUPS[g]
        for copy in second[g]:
            copy.wait_recv()
        part1[0, lo:hi] = part1[0, lo:hi] + whole1[0, lo:hi] + whole1[1, lo:hi]

    def hop_a(s):
        for half in (0, 1):
            lo, hi = 2 * half, 2 * half + 2
            pair = pl.ds(lo, 2)
            for k, (way, last) in enumerate(WAYS):
                if s > last:
                    continue
                there = me.zat(way * (last - s))
                if s == 0:
                    ring["a", way, 0, half] = w.go(part0.at[there, pair], rb0.at[k, 0, pair], me.zdev(way))
                    continue
                ring["a", way, s - 1, half].wait_recv()
                if s < last:
                    rb0[k, s - 1, lo:hi] = rb0[k, s - 1, lo:hi] + part0[there, lo:hi]
                    ring["a", way, s, half] = w.go(rb0.at[k, s - 1, pair], rb0.at[k, s, pair], me.zdev(way))

    def hop_b(s):
        for k, (way, last) in enumerate(WAYS):
            if s > last:
                continue
            slot = FAR.index(way * (last - s))
            if s == 0:
                ring["b", way, 0] = w.go(part1.at[0, slot], rb1.at[k, 0], me.zdev(way))
                continue
            ring["b", way, s - 1].wait_recv()
            if s < last:
                rb1[k, s - 1] = rb1[k, s - 1] + part1[0, slot]
                ring["b", way, s] = w.go(rb1.at[k, s - 1], rb1.at[k, s], me.zdev(way))

    fill1(2)
    for g in range(4):
        begin(g)
    fill0()
    copies = []
    for s in range(11):
        if s <= 8:
            hop_a(s)
        if s == 0:
            fill1(1)
            fill1(3)
        if s == 1:
            fill1(0)
        if s == 8:
            rb0[0, 7] = rb0[0, 7] + part0[me.z] + rb0[1, 6]
            copies = [w.go(rb0.at[0, 7, e], xb0.at[e], me.xdev(e)) for e in (2, 1, 3)]
        if s in (0, 2, 4, 6):
            pass_on(s // 2)
        if s in (1, 3, 5, 7):
            collect(s // 2)
        if s >= 2:
            hop_b(s - 2)
        beside(s)
        w.drain(64)
    for copy in copies:
        copy.wait_recv()
    return rb0[0, 7, 0] + xb0[1] + xb0[2] + xb0[3], part1[0, 15] + rb1[0, 7] + rb1[1, 6]


QUARTERS = ((0, 0), (0, 1), (1, 1), (1, 0))


def sum_gram(me, w, product, gs, gfull, zbuf, xbuf):
    gram = dot(product, product, ((0,), (0,)))
    for n, (r, h) in enumerate(QUARTERS):
        gs[n] = gram[r * HALF : (r + 1) * HALF, h * HALF : (h + 1) * HALF].reshape(HALF // 8, 8, HALF)

    def tile(ref, z):
        return ref.at[lax.div(z, 4), me.y * 4 + lax.rem(z, 4)]

    far = [8] + [d for r in range(7, 0, -1) for d in (r, ZS - r)]
    copies = [w.go(tile(gs, me.zat(d)), zbuf.at[d], me.zdev(d)) for d in far]
    yield
    total = gs[lax.div(me.z, 4), me.y * 4 + lax.rem(me.z, 4)]
    for d, copy in reversed(list(zip(far, copies))):
        copy.wait_recv()
        total = total + zbuf[d]
    xbuf[me.x] = total
    copies = [w.go(xbuf.at[me.x], xbuf.at[me.x], me.xdev(d)) for d in (2, 1, 3)]
    yield
    for copy in copies:
        copy.wait_recv()
    gfull[lax.div(me.z, 4), me.y * 4 + lax.rem(me.z, 4)] = xbuf[0] + xbuf[1] + xbuf[2] + xbuf[3]
    copies = [w.go(tile(gfull, me.z), tile(gfull, me.z), me.zdev(d)) for d in far]
    yield
    for copy in reversed(copies):
        copy.wait_recv()
    mine = gfull.at[pl.ds(0, 3), pl.ds(me.y * 4, 4)]
    copies = [w.go(mine, mine, me.ydev(d)) for d in (2, 1, 3)]
    yield
    for copy in copies:
        copy.wait_recv()


def kernel(grad, mom, basis, new_mom, new_basis, update,
           gbuf, mbuf, bfull0, bslots1, bfull1, part, rs, q, p1, p2, a, w1, w2, turned,
           gs, gfull, zbuf, xbuf, gs2, gfull2, zbuf2, xbuf2,
           part0, part1, tmp, full0, slots1, full1, rb0, xb0, rb1, half1, whole1, cols0, cols1, sq, out,
           send, recv, local):
    me = Place()
    w = Wires(send, recv)
    loads = [pltpu.make_async_copy(grad, gbuf, local.at[0]), pltpu.make_async_copy(mom, mbuf, local.at[1])]
    for load in loads:
        load.start()
    greet([me.zdev(d) for d in range(1, ZS)] + [me.xdev(d) for d in range(1, XS)] + [me.tdev(d) for d in range(1, TP)])

    share = part.shape[2]

    def multiply(l):
        total = jnp.zeros((part.shape[1] * share, RANK), F32)
        for e in range(XS):
            total = total + dot(gbuf[l, :, me.cols(e)], gathered(bfull0, bfull1, l, e), ((1,), (0,)))
        part[l] = total.reshape(part.shape[1], share, RANK)

    def beside_basis(s):
        if s == 0:
            for load in loads:
                load.wait()
            gbuf[...] = gbuf[...] + mbuf[...]
        if s in (1, 2):
            turned[s - 1] = gbuf[s - 1].T
        if s == 9:
            multiply(0)

    gather_plane(me, w, basis[0], basis[1], bfull0, bslots1, bfull1, beside_basis)
    multiply(1)
    copies = []
    away = (4, 3, 5, 2, 6, 1, 7)
    for d in away:
        there = lax.rem(me.t + d, TP)
        copies.append(w.go(part.at[lax.rem(there, CS), lax.div(there, CS)], rs.at[d], me.tdev(d)))
    total = part[me.c, me.y]
    for d, copy in zip(away, copies):
        copy.wait_recv()
        total = total + rs[d]
    q[me.c, me.y] = total
    copies = [w.go(q.at[me.c, me.y], q.at[me.c, me.y], me.ydev(d)) for d in (2, 1, 3)]
    for copy in copies:
        copy.wait_recv()
    swap = w.go(q.at[me.c], q.at[me.c], me.cdev())

    def take(gram):
        for n, (r, h) in enumerate(QUARTERS):
            quarter = gram[n].reshape(HALF, HALF) if n < 3 else jnp.zeros((HALF, HALF), F32)
            a[r * HALF : (r + 1) * HALF, h * HALF : (h + 1) * HALF] = quarter

    sums = [sum_gram(me, w, q[me.c].reshape(YS * share, RANK), gs, gfull, zbuf, xbuf)]
    next(sums[0])
    swap.wait_recv()
    trade = []

    def fill0():
        for e in range(XS):
            cols = dot(turned[0, me.cols(e)], q[0].reshape(YS * share, RANK), ((1,), (0,)))
            part0[:, e] = cols.reshape(ZS, 16, RANK)

    def fill1(e):
        cols = dot(turned[1, me.cols(e)], q[1].reshape(YS * share, RANK), ((1,), (0,)))
        tmp[...] = cols.reshape(ZS, 16, RANK)
        for slot, d in enumerate(FAR):
            part1[e, slot] = tmp[me.zat(d)]

    def beside_scatter(s):
        if s in (1, 2, 4, 6):
            next(sums[0], None)
        if s == 10:
            next(sums[1])
        if s == 6:
            take(gfull)
        for n in {6: (0, 1), 7: (2, 3, 4), 8: (5, 6, 7)}.get(s, ()):
            eliminate(a, w1.at[me.c], n * PANEL)
        if s == 8:
            trade.append(w.go(w1.at[me.c], w1.at[me.c], me.cdev()))
            p1[...] = dot(q[me.c].reshape(YS * share, RANK), w1[me.c], ((1,), (1,)))
            sums.append(sum_gram(me, w, p1[...], gs2, gfull2, zbuf2, xbuf2))
            next(sums[1])

    def beside_gather(s):
        if s in (0, 2, 4):
            next(sums[1], None)
        if s == 4:
            take(gfull2)
        for n in {4: (0, 1, 2), 5: (3, 4, 5), 6: (6, 7)}.get(s, ()):
            eliminate(a, w2.at[me.c], n * PANEL)
        if s == 6:
            trade.append(w.go(w2.at[me.c], w2.at[me.c], me.cdev()))
            p2[me.c] = dot(p1[...], w2[me.c], ((1,), (1,)))
            trade.append(w.go(p2.at[me.c], p2.at[me.c], me.cdev()))
        if s == 9:
            for copy in trade[1:]:
                copy.wait_recv()
            finish(0)

    def finish(l):
        squares = jnp.zeros((1, RANK), F32)
        for e in range(XS):
            block = dot3(gathered(full0, full1, l, e), w2[l], 1)
            if l == 0:
                cols0[:, e] = block.reshape(ZS, 16, RANK)
            else:
                cols1[e] = block.reshape(ZS, 16, RANK)
            squares = squares + jnp.sum(block * block, 0, keepdims=True)
        sq[me.t, l] = jnp.broadcast_to(squares, (8, RANK))

    own = scatter_plane(me, w, part0, part1, rb0, xb0, rb1, half1, whole1, fill0, fill1, beside_scatter)
    trade[0].wait_recv()
    own = [dot(own[l], w1[l], ((1,), (1,))) for l in range(LAYERS)]
    gather_plane(me, w, own[0], own[1], full0, slots1, full1, beside_gather)
    finish(1)
    stores = []
    copies = [w.go(sq.at[me.t], sq.at[me.t], me.tdev(d)) for d in range(1, TP)]
    for l in range(LAYERS):
        for e in range(XS):
            block = gathered(cols0, cols1, l, e)
            mbuf[l, :, me.cols(e)] = gbuf[l, :, me.cols(e)] - (1.0 - keep_rate) * dot3(p2[l], block, 1)
        stores.append(pltpu.make_async_copy(mbuf.at[l], new_mom.at[l], local.at[2 + l]))
        stores[-1].start()
    for copy in copies:
        copy.wait_recv()
    for l in range(LAYERS):
        squares = sq[0, l]
        for t in range(1, TP):
            squares = squares + sq[t, l]
        norm = jnp.sqrt(squares[0:1] + eps)
        new_basis[l] = (cols0[me.z, 0] if l == 0 else cols1[0, me.z]) / norm
        scaled = p2[l] * (math.sqrt(ROWS * COLS / RANK) / norm)
        for e in range(XS):
            out[l, :, me.cols(e)] = dot3(scaled, gathered(cols0, cols1, l, e), 1)
        stores.append(pltpu.make_async_copy(out.at[l], update.at[l], local.at[4 + l]))
        stores[-1].start()
    w.drain()
    for store in stores:
        store.wait()


PANEL = 32


def split3(a):
    high = a.astype(BF16)
    rest = a - high.astype(F32)
    mid = rest.astype(BF16)
    low = (rest - mid.astype(F32)).astype(BF16)
    return high, mid, low


def eliminate(a_ref, w_ref, r0):
    halves = [a_ref[r0 : r0 + PANEL, h * HALF : (h + 1) * HALF] for h in (0, 1)]
    finished = []
    for j0 in range(r0, r0 + PANEL, 8):
        side, start = divmod(j0, HALF)
        height = r0 + PANEL - j0
        lane = lax.broadcasted_iota(jnp.int32, (height, HALF), 1)
        row = lax.broadcasted_iota(jnp.int32, (height, HALF), 0)
        cols = [jnp.broadcast_to(halves[side][:, start + k : start + k + 1], (height, HALF)) for k in range(8)]
        scale = jnp.zeros((8, HALF), F32)
        for k in range(8):
            pivot = cols[k][k : k + 1]
            ratio = jnp.where(row > k, cols[k] * (1.0 / pivot), 0.0)
            scale = jnp.where(row[:8] == k, lax.rsqrt(pivot), scale)
            for n in range(k + 1, 8):
                cols[n] = cols[n] - ratio * cols[n][k : k + 1]
            for h in (0, 1):
                kept, spread = halves[h], halves[h][k : k + 1]
                if h == side:
                    spread = jnp.where(lane[0:1] == start + k, 1.0, spread)
                    kept = jnp.where((lane == start + k) & (row >= k), jnp.where(row == k, 1.0, 0.0), kept)
                halves[h] = kept - ratio * spread
        finished.append([half[:8] * scale for half in halves])
        halves = [half[8:] for half in halves] if height > 8 else None
    whole = jnp.concatenate([jnp.concatenate(rows, 1) for rows in finished], 0)
    lanes = lax.broadcasted_iota(jnp.int32, (PANEL, RANK), 1)
    rows = lax.broadcasted_iota(jnp.int32, (PANEL, RANK), 0) + r0
    w_ref[r0 : r0 + PANEL, :] = jnp.where(lanes <= rows, whole, 0.0)
    rest = r0 + PANEL
    if rest < RANK:
        right = jnp.where((lanes > rows) & (lanes < rest), 0.0, whole)
        h, m, l = split3(whole)
        hr, mr, lr = split3(right)
        left = jnp.concatenate([h, h, m, h, l, m], 0)
        base = rest // HALF * HALF
        change = lax.dot_general(
            left[:, base:], jnp.concatenate([hr, mr, hr, lr, hr, mr], 0),
            (((0,), (0,)), ((), ())), preferred_element_type=F32)
        wide = lax.broadcasted_iota(jnp.int32, (RANK - rest, RANK), 1)
        old = jnp.where((wide >= r0) & (wide < rest), 0.0, a_ref[rest:, :])
        a_ref[rest:, :] = old - change[rest - base :, :]


def hand_over(a, b, c, a_out, b_out, c_out):
    a_out[...] = a[...]
    b_out[...] = b[...]
    c_out[...] = c[...]


def vmem(*shape):
    return pltpu.VMEM(shape, F32)


V = pl.BlockSpec(memory_space=pltpu.VMEM)
ANY = pl.BlockSpec(memory_space=pl.ANY)
COPIES = 288


def per_device(gradient, momentum, basis):
    rows, cols = gradient.shape[1:]
    share = basis.shape[1]
    whole = jax.ShapeDtypeStruct((LAYERS, rows, cols), F32)
    plane = [vmem(ZS, XS, share, RANK), vmem(XS, ZS, share, RANK), vmem(XS, ZS, share, RANK)]
    sums = [vmem(4, HALF // 8, 8, HALF), vmem(4, HALF // 8, 8, HALF), vmem(ZS, 8, HALF), vmem(XS, 8, HALF)]
    shapes = (whole, jax.ShapeDtypeStruct((LAYERS, share, RANK), F32), whole)
    results = pl.pallas_call(
        kernel,
        out_shape=shapes,
        in_specs=[ANY, ANY, V],
        out_specs=(ANY, V, ANY),
        scratch_shapes=[
            vmem(LAYERS, rows, cols), vmem(LAYERS, rows, cols), *plane,
            vmem(LAYERS, YS, rows // YS, RANK), vmem(TP, rows // YS, RANK), vmem(LAYERS, YS, rows // YS, RANK),
            vmem(rows, RANK), vmem(LAYERS, rows, RANK),
            vmem(RANK, RANK), vmem(LAYERS, RANK, RANK), vmem(LAYERS, RANK, RANK), vmem(LAYERS, cols, rows),
            *sums, *sums,
            vmem(ZS, XS, share, RANK), vmem(XS, ZS, share, RANK), vmem(ZS, share, RANK), *plane,
            vmem(2, 8, XS, share, RANK), vmem(XS, share, RANK), vmem(2, 8, share, RANK),
            vmem(ZS, share, RANK), vmem(2, ZS, share, RANK),
            vmem(ZS, XS, share, RANK), vmem(XS, ZS, share, RANK), vmem(TP, LAYERS, 8, RANK), vmem(LAYERS, rows, cols),
            pltpu.SemaphoreType.DMA((COPIES,)), pltpu.SemaphoreType.DMA((COPIES,)), pltpu.SemaphoreType.DMA((6,)),
        ],
        compiler_params=pltpu.CompilerParams(
            collective_id=0, has_side_effects=True, vmem_limit_bytes=60 * 2**20),
        name="step",
    )(gradient, momentum, basis)
    return pl.pallas_call(
        hand_over,
        out_shape=shapes,
        grid=(LAYERS,),
        in_specs=[pl.BlockSpec((1,) + shape.shape[1:], lambda l: (l, 0, 0)) for shape in shapes],
        out_specs=tuple(pl.BlockSpec((1,) + shape.shape[1:], lambda l: (l, 0, 0)) for shape in shapes),
        compiler_params=pltpu.CompilerParams(vmem_limit_bytes=60 * 2**20),
        name="hand_over",
    )(*results)


def solution(mesh):
    return jax.shard_map(
        per_device,
        mesh=mesh,
        in_specs=(P(None, "fsdp", "tp"), P(None, "fsdp", "tp"), P(None, ("tp", "fsdp"), None)),
        out_specs=(P(None, "fsdp", "tp"), P(None, ("tp", "fsdp"), None), P(None, "fsdp", "tp")),
        check_vma=False,
    )
```
